32 devices in a mesh: rows: 8 (over y, x, core), feat: 4 (over z).
Axes of the slice: x: 2, y: 2, z: 4, core: 2. Of those that a mesh axis runs over, the one named last changes fastest.
Arguments:
- features: bfloat16 [2048, 512], P('rows', 'feat'), may hold values from -6 to 6
- weight: bfloat16 [512, 512], P(None, 'feat'), may hold values from -0.25 to 0.25
- block_values: bfloat16 [16, 8, 128, 128], P('rows', 'feat'), may hold values from -0.25 to 0.25
- columns: int32 [16, 8], P('rows'), may hold values from 0 to 15, as said below
- counts: int32 [16], P('rows'), may hold values from 2 to 8, as said below
- cotangent: bfloat16 [2048, 512], P('rows', 'feat'), may hold values from -6 to 6
Outputs:
- hidden: bfloat16 [2048, 512], P('rows', 'feat')
- grad_features: bfloat16 [2048, 512], P('rows', 'feat')
- grad_weight: float32 [512, 512], P(None, 'feat')
The draws below stay inside these ranges and needn't reach their ends.
Inputs may be any that keep to these rules, and one draw needn't show every extreme that they name: `columns`: the 8 column blocks of a row block are distinct and lie on the devices within 2 indices of the row block's own index along rows, counted around the axis (the device of block c is c // 2). Slots 0 to counts[g] - 1 of row block g are live, the others are ignored; some row block has exactly 8 live slots.
All inputs are finite; a program needn't handle non-finite values.
Results may differ from the reference program's by a relative error of at most 0.0067.
Values may be sent and summed in bfloat16 or wider, within the bound.
A program may use at most 64 MiB of HBM per device.

```python
import jax
import jax.numpy as jnp
from jax import lax

F = 512
O = 512
FB = 128
RB = 2
S = 8
REACH = 2
NRB = 16
NODES = 2048
N_ROWS = 8


def draw_columns(key, part):
    window_span = (2 * REACH + 1) * RB
    devices = NRB // RB
    scores = jax.random.randint(key, (NRB, window_span), 0, 1 << 20) * window_span + jnp.arange(window_span)
    chosen = lax.top_k(scores, S)[1]
    owner_dev = jnp.arange(NRB)[:, None] // RB
    target = (owner_dev + chosen // RB - REACH + devices) % devices
    return (target * RB + chosen % RB).astype(jnp.int32)


def draw_counts(key, part):
    devices = NRB // RB
    level_key = jax.random.fold_in(key, 11)
    count_key = jax.random.fold_in(key, 12)
    pick_key = jax.random.fold_in(key, 13)
    levels = jax.random.randint(level_key, (devices,), 0, 5)
    ceiling = 2 + (S - 2) * levels * levels // 16
    ceiling_rows = jnp.repeat(ceiling, RB)
    raw_draw = jax.random.randint(count_key, (NRB,), 0, 1 << 20)
    drawn = 2 + raw_draw % (ceiling_rows - 1)
    special = jax.random.randint(pick_key, (), 0, NRB)
    return jnp.where(jnp.arange(NRB) == special, S, drawn).astype(jnp.int32)


def shard_levels(key, extent, split, least, high):
    loudness = 1.0
    for axis_at, shards_of in split:
        draws = jax.random.uniform(jax.random.fold_in(jax.random.fold_in(key, 6), axis_at), (shards_of,), jnp.float32, least / len(split), high / len(split))
        loudness = loudness * jnp.repeat(jnp.exp(draws), extent[axis_at] // shards_of).reshape((-1,) + (1,) * (len(extent) - 1 - axis_at))
    return loudness


def gaussian(own_key, extent, scale, most, shards=(), held_as=jnp.bfloat16):
    level = shard_levels(own_key, extent, shards, -0.22, 0.18) if shards else 1.0
    result = jax.random.normal(own_key, extent, jnp.float32) * scale * level
    return jnp.minimum(jnp.maximum(result, -most), most).astype(held_as)


def setup_inputs(seed: int = 0) -> dict:
    splits = jax.random.split(jax.random.key(seed), 7)
    return {
        "features": gaussian(splits[0], (NODES, F), 1.0, 6.0, ((0, 8), (1, 4))),
        "weight": gaussian(splits[1], (F, O), F ** -0.5, 0.25, ((1, 4),)),
        "block_values": gaussian(splits[2], (NRB, S, FB, FB), (FB * S // 2) ** -0.5, 0.25, ((0, 8), (1, 4))),
        "columns": draw_columns(jax.random.fold_in(splits[6], 71), 0),
        "counts": draw_counts(jax.random.fold_in(splits[6], 71), 0),
        "cotangent": gaussian(splits[5], (NODES, O), 1.0, 6.0, ((0, 8), (1, 4))),
    }


def activation(values):
    return jax.nn.gelu(values, approximate=True)

def reference(features, weight, block_values, columns, counts, cotangent):
    row_total = counts.shape[0]
    block_size = block_values.shape[2]
    in_width = features.shape[1]
    feat_blocks = features.reshape(row_total, block_size, in_width)
    summed = jnp.zeros((row_total, block_size, in_width), jnp.float32)
    for slot_index in range(S):
        slot_live = (counts > slot_index).astype(jnp.float32)[:, None, None]
        picked = jnp.take(feat_blocks, columns[:, slot_index], axis=0).astype(jnp.float32)
        values_now = block_values[:, slot_index].astype(jnp.float32) * slot_live
        summed = summed + jnp.einsum('gij,gjf->gif', values_now, picked)
    aggregated = summed.reshape(NODES, in_width).astype(jnp.bfloat16)
    pre_act = jnp.dot(aggregated, weight, preferred_element_type=jnp.float32)
    hidden, act_grad = jax.vjp(activation, pre_act)
    grad_pre = act_grad(cotangent.astype(jnp.float32))[0].astype(jnp.bfloat16)
    grad_weight = lax.dot_general(aggregated, grad_pre, (((0,), (0,)), ((), ())), preferred_element_type=jnp.float32)
    grad_weight = grad_weight * float(NODES) ** (-0.5)
    grad_agg = lax.dot_general(grad_pre, weight, (((1,), (1,)), ((), ())), preferred_element_type=jnp.float32).astype(jnp.bfloat16)
    grad_blocks = grad_agg.reshape(row_total, block_size, in_width).astype(jnp.float32)
    span_count = 2 * REACH + 1
    center_mask = (jnp.arange(span_count) == REACH)[:, None, None, None]
    slot_ids = jnp.arange(S).astype(jnp.int32)

    def device_term(device, total):
        device = jnp.asarray(device).astype(jnp.int32)
        first = (device * RB).astype(jnp.int32)
        values_dev = lax.dynamic_slice_in_dim(block_values, first, RB, 0).astype(jnp.float32)
        cols_dev = lax.dynamic_slice_in_dim(columns, first, RB, 0).astype(jnp.int32)
        count_dev = lax.dynamic_slice_in_dim(counts, first, RB, 0).astype(jnp.int32)
        live = (slot_ids[None, :] < count_dev[:, None]).astype(jnp.float32)
        values_dev = values_dev * live[:, :, None, None]
        grads_dev = lax.dynamic_slice_in_dim(grad_blocks, first, RB, 0)
        products = jnp.einsum('gsij,gif->gsjf', values_dev, grads_dev)
        offsets = ((cols_dev // RB - device + REACH + N_ROWS) % N_ROWS).astype(jnp.int32)
        places = (offsets * RB + cols_dev % RB).astype(jnp.int32)
        window_sum = jnp.zeros((span_count * RB, block_size, in_width), jnp.float32)
        window_sum = window_sum.at[places.reshape(-1)].add(products.reshape(-1, block_size, in_width))
        window_sum = window_sum.reshape(span_count, RB, block_size, in_width)
        rounded = lax.optimization_barrier(window_sum.astype(jnp.bfloat16)).astype(jnp.float32)
        window_sum = jnp.where(center_mask, window_sum, rounded)
        owners = ((device + jnp.arange(span_count).astype(jnp.int32) - REACH + N_ROWS) % N_ROWS).astype(jnp.int32)
        targets = (owners[:, None] * RB + jnp.arange(RB).astype(jnp.int32)[None, :]).astype(jnp.int32)
        return total.at[targets.reshape(-1)].add(window_sum.reshape(-1, block_size, in_width))
    spread = lax.fori_loop(0, N_ROWS, device_term, jnp.zeros((row_total, block_size, in_width), jnp.float32))
    grad_features = spread.reshape(NODES, in_width).astype(jnp.bfloat16)
    return (hidden.astype(jnp.bfloat16), grad_features, grad_weight)
```

```python
import functools

import jax
import jax.numpy as jnp
from jax import lax
from jax.experimental import pallas as pl
from jax.experimental.pallas import tpu as pltpu
from jax.sharding import PartitionSpec as P

MESH = pl.DeviceIdType.MESH
F32 = jnp.float32
BF16 = jnp.bfloat16
GELU_SCALE = 0.7978845608028654
GELU_CUBE = 0.044715


def gelu_and_slope(v):
    square = v * v
    t = jnp.tanh(GELU_SCALE * (v + GELU_CUBE * (square * v)))
    half = 0.5 * (1.0 + t)
    inner = GELU_SCALE * (1.0 + 3.0 * GELU_CUBE * square)
    return v * half, half + 0.5 * v * (1.0 - t * t) * inner


def dot(a, b, contract):
    return lax.dot_general(a, b, (contract, ((), ())), preferred_element_type=F32)


def kernel(n, m, reach, rb, sl, in_sum, cols, cnt, x_ref, w_ref, t_ref, ct_ref,
           hid_ref, gf_ref, gw_ref, xall, wrow, tl, yw, sw, sr, gall, gpart, gwp, gwr, gwa,
           send_sem, recv_sem):
    r = lax.axis_index("rows")
    f = lax.axis_index("feat")
    fb = t_ref.shape[1]
    rows = rb * fb
    fw = x_ref.shape[1]
    per = rb * sl
    chunk = gwr.shape[1]
    halo = [o for d in range(1, reach + 1) for o in (d, -d)]
    feat_d = list(range(1, m))
    row_d = list(range(1, n)) if in_sum else []
    row_peers = [d % n for d in (row_d if in_sum else halo)]

    barrier = pltpu.get_barrier_semaphore()
    for d in feat_d:
        pl.semaphore_signal(barrier, inc=1, device_id={"feat": lax.rem(f + d, m)}, device_id_type=MESH)
    for d in row_peers:
        pl.semaphore_signal(barrier, inc=1, device_id={"rows": lax.rem(r + d, n)}, device_id_type=MESH)
    pl.semaphore_wait(barrier, len(feat_d) + len(row_peers))

    started = []

    def push(src, dst, axis, peer):
        at = len(started)
        copy = pltpu.make_async_remote_copy(
            src_ref=src, dst_ref=dst, send_sem=send_sem.at[at], recv_sem=recv_sem.at[at],
            device_id={axis: peer}, device_id_type=MESH)
        copy.start()
        started.append(copy)
        return copy

    x_in = {d: push(x_ref, xall.at[d], "feat", lax.rem(f + d, m)) for d in feat_d}
    t_in = {d: push(t_ref, tl.at[pl.ds(d * per, per)], "feat", lax.rem(f + d, m)) for d in feat_d}
    w_in = {}
    for d in feat_d:
        peer = lax.rem(f + d, m)
        w_in[d] = push(w_ref.at[pl.ds(pl.multiple_of(peer * fw, fw), fw)], wrow.at[d], "feat", peer)

    source = [lax.rem(f + m - d, m) for d in range(m)]

    def weight_rows(d):
        return w_ref[pl.ds(pl.multiple_of(source[d] * fw, fw), fw), :]

    zero_tile = m * per
    place = {}
    for d in range(m):
        for g in range(rb):
            for j in range(sl):
                s = source[d] * sl + j
                col = cols[g, s]
                offset = lax.rem(lax.div(col, rb) - r + reach + n, n)
                live = cnt[g] > s
                at = (d * rb + g) * sl + j
                place[at] = (g, live, offset * rb + lax.rem(col, rb))
    inverse = {}
    for c in range((2 * reach + 1) * rb):
        for g in range(rb):
            found = jnp.int32(zero_tile)
            for at, (group, live, where) in place.items():
                if group == g:
                    found = jnp.where(jnp.logical_and(live, where == c), at, found)
            inverse[c, g] = found

    tl[pl.ds(0, per)] = t_ref[...]
    tl[zero_tile] = jnp.zeros((fb, fb), BF16)

    order = [d for pair in zip(range(1, m), range(m - 1, 0, -1)) for d in pair]
    order = list(dict.fromkeys(order))
    total = dot(x_ref[...], weight_rows(0), ((1,), (0,)))
    for d in order:
        x_in[d].wait_recv()
        total = total + dot(xall[d], weight_rows(d), ((1,), (0,)))
    yw[pl.ds(reach * rb, rb)] = total.astype(BF16).reshape(rb, fb, fw)
    y_in = [push(yw.at[pl.ds(reach * rb, rb)], yw.at[pl.ds((reach - o) * rb, rb)], "rows",
                 lax.rem(r + o + n, n)) for o in halo]
    for copy in y_in:
        copy.wait_recv()

    sums = [jnp.zeros((fb, fw), F32) for _ in range(rb)]
    for d in [0] + order:
        if d:
            t_in[d].wait_recv()
        for g in range(rb):
            for j in range(sl):
                at = (d * rb + g) * sl + j
                _, live, where = place[at]
                product = dot(tl[at], yw[jnp.minimum(where, yw.shape[0] - 1)], ((1,), (0,)))
                sums[g] = sums[g] + jnp.where(live, product, 0.0)
    pre = jnp.concatenate(sums, axis=0)
    hidden, slope = gelu_and_slope(pre)
    grad_pre = (ct_ref[...].astype(F32) * slope).astype(BF16)

    def piece(o):
        first = (reach + o) * rb
        parts = []
        for c in range(first, first + rb):
            tiles = jnp.concatenate([tl[inverse[c, g]] for g in range(rb)], axis=0)
            parts.append(dot(tiles, grad_pre, ((0,), (0,))))
        return jnp.concatenate(parts, axis=0)

    s_in = []
    for at, o in enumerate(reversed(halo)):
        sw[at] = piece(o).astype(BF16)
        s_in.append(push(sw.at[at], sr.at[at], "rows", lax.rem(r + o + n, n)))
    grad = piece(0)
    hid_ref[...] = hidden.astype(BF16)
    for at, copy in enumerate(s_in):
        copy.wait_recv()
        grad = grad + sr[at].astype(F32)
    gall[0] = grad.astype(BF16)
    g_in = {d: push(gall.at[0], gall.at[d], "feat", lax.rem(f + d, m)) for d in feat_d}

    for d in range(m):
        term = dot(xall[d] if d else x_ref[...], gall[0], ((0,), (0,)))
        at = pl.ds(pl.multiple_of(source[d] * fw, fw), fw)
        gpart[at, :] = term
        gwp[at, :] = term.astype(BF16)
    scale = float(rows * n) ** -0.5
    if in_sum:
        def chunk_of(d):
            return pl.ds(pl.multiple_of(lax.rem(r + n + d, n) * chunk, chunk), chunk)

        gw_in = {d: push(gwp.at[chunk_of(d)], gwr.at[d], "rows", lax.rem(r + d, n)) for d in row_d}
        part = gpart[chunk_of(0), :]
        for d in row_d:
            gw_in[d].wait_recv()
            part = part + gwr[d].astype(F32)
        gwa[0] = (part * scale).astype(BF16)
        all_in = {d: push(gwa.at[0], gwa.at[d], "rows", lax.rem(r + d, n)) for d in row_d}
    else:
        gw_ref[...] = gpart[...] * scale

    for d in feat_d:
        w_in[d].wait_recv()
    out = dot(gall[0], weight_rows(0), ((1,), (1,)))
    for d in order:
        g_in[d].wait_recv()
        out = out + dot(gall[d], wrow[d], ((1,), (1,)))
    gf_ref[...] = out.astype(BF16)
    if in_sum:
        gw_ref[chunk_of(0), :] = gwa[0].astype(F32)
        for d in row_d:
            all_in[d].wait_recv()
            gw_ref[chunk_of(-d), :] = gwa[d].astype(F32)
    for copy in started:
        copy.wait_send()


def on_device(features, weight, block_values, columns, counts, cotangent):
    n = lax.axis_size("rows")
    m = lax.axis_size("feat")
    reach = min(4, (n - 1) // 3)
    rb, sl, fb, _ = block_values.shape
    rows, fw = features.shape
    depth = weight.shape[0]
    in_sum = depth % (n * 16) == 0
    chunk = depth // n if in_sum else 16
    span = 2 * reach + 1
    copies = 4 * (m - 1) + 4 * reach + (2 * (n - 1) if in_sum else 0)
    vmem = pl.BlockSpec(memory_space=pltpu.VMEM)
    smem = pl.BlockSpec(memory_space=pltpu.SMEM)
    hidden, grad_features, grad_weight = pl.pallas_call(
        functools.partial(kernel, n, m, reach, rb, sl, in_sum),
        out_shape=(
            jax.ShapeDtypeStruct((rows, fw), BF16),
            jax.ShapeDtypeStruct((rows, fw), BF16),
            jax.ShapeDtypeStruct((depth, fw), F32),
        ),
        in_specs=[smem, smem, vmem, vmem, vmem, vmem],
        out_specs=(vmem, vmem, vmem),
        scratch_shapes=[
            pltpu.VMEM((m, rows, fw), BF16),
            pltpu.VMEM((m, fw, fw), BF16),
            pltpu.VMEM((m * rb * sl + 1, fb, fb), BF16),
            pltpu.VMEM((span * rb, fb, fw), BF16),
            pltpu.VMEM((2 * reach, rows, fw), BF16),
            pltpu.VMEM((2 * reach, rows, fw), BF16),
            pltpu.VMEM((m, rows, fw), BF16),
            pltpu.VMEM((depth, fw), F32),
            pltpu.VMEM((depth, fw), BF16),
            pltpu.VMEM((n if in_sum else 1, chunk, fw), BF16),
            pltpu.VMEM((n if in_sum else 1, chunk, fw), BF16),
            pltpu.SemaphoreType.DMA((copies,)),
            pltpu.SemaphoreType.DMA((copies,)),
        ],
        compiler_params=pltpu.CompilerParams(
            collective_id=0, has_side_effects=True, vmem_limit_bytes=32 * 1024 * 1024),
    )(columns, counts, features, weight, block_values.reshape(rb * sl, fb, fb), cotangent)
    if not in_sum:
        grad_weight = lax.psum(grad_weight, "rows")
    return hidden, grad_features, grad_weight


def solution(mesh):
    in_specs = (
        P("rows", "feat"),
        P(None, "feat"),
        P("rows", "feat", None, None),
        P("rows", None),
        P("rows"),
        P("rows", "feat"),
    )
    out_specs = (P("rows", "feat"), P("rows", "feat"), P(None, "feat"))
    return jax.shard_map(
        on_device, mesh=mesh, in_specs=in_specs, out_specs=out_specs, check_vma=False
    )
```

```python
import functools

import jax
import jax.numpy as jnp
from jax import lax
from jax.experimental import pallas as pl
from jax.experimental.pallas import tpu as pltpu
from jax.sharding import PartitionSpec as P

MESH = pl.DeviceIdType.MESH
F32 = jnp.float32
BF16 = jnp.bfloat16
GELU_SCALE = 0.7978845608028654
GELU_CUBE = 0.044715


def gelu_and_slope(v):
    square = v * v
    t = jnp.tanh(GELU_SCALE * (v + GELU_CUBE * (square * v)))
    half = 0.5 * (1.0 + t)
    inner = GELU_SCALE * (1.0 + 3.0 * GELU_CUBE * square)
    return v * half, half + 0.5 * v * (1.0 - t * t) * inner


def dot(a, b, contract):
    return lax.dot_general(a, b, (contract, ((), ())), preferred_element_type=F32)


def nearest_first(f, m):
    tables = []
    for me in range(m):
        line = [p for e in range(1, m) for p in (me - e, me + e) if 0 <= p < m]
        tables.append(line)
    steps = []
    for i in range(m - 1):
        at = jnp.int32(tables[0][i])
        for me in range(1, m):
            at = jnp.where(f == me, tables[me][i], at)
        steps.append(at)
    return steps


def kernel(n, m, reach, rb, sl, in_sum, cols_hbm, cnt_hbm, x_hbm, w_hbm, t_hbm, ct_hbm,
           hid_hbm, gf_hbm, gw_hbm, hid_ref, gf_ref, gw_ref, xall, w_ref, ct_ref, wrow, tl, yw, sw, sr, gall, gpart, gwp, gwr, gwa,
           send_sem, recv_sem, hop_send, hop_recv, load_sem, save_sem, cols, cnt):
    r = lax.axis_index("rows")
    f = lax.axis_index("feat")
    fb = t_hbm.shape[1]
    rows, fw = x_hbm.shape
    per = rb * sl
    chunk = gwr.shape[1]
    halo = [o for d in range(1, reach + 1) for o in (d, -d)]
    feat_d = list(range(1, m))
    row_d = list(range(1, n)) if in_sum else []
    row_peers = [d % n for d in (row_d if in_sum else halo)]

    def shard(s):
        return tl.at[pl.ds(s * per, per)]

    def rows_of(s):
        return pl.ds(pl.multiple_of(s * fw, fw), fw)

    loads = [
        pltpu.make_async_copy(x_hbm, xall.at[f], load_sem.at[0]),
        pltpu.make_async_copy(w_hbm, w_ref, load_sem.at[1]),
        pltpu.make_async_copy(t_hbm, shard(f), load_sem.at[2]),
        pltpu.make_async_copy(ct_hbm, ct_ref, load_sem.at[3]),
        pltpu.make_async_copy(w_hbm.at[rows_of(f)], wrow.at[f], load_sem.at[4]),
        pltpu.make_async_copy(cols_hbm, cols, load_sem.at[5]),
        pltpu.make_async_copy(cnt_hbm, cnt, load_sem.at[6]),
    ]
    for load in loads:
        load.start()

    barrier = pltpu.get_barrier_semaphore()
    for d in feat_d:
        pl.semaphore_signal(barrier, inc=1, device_id={"feat": lax.rem(f + d, m)}, device_id_type=MESH)
    for d in row_peers:
        pl.semaphore_signal(barrier, inc=1, device_id={"rows": lax.rem(r + d, n)}, device_id_type=MESH)
    pl.semaphore_wait(barrier, len(feat_d) + len(row_peers))

    started = []

    def push(src, dst, axis, peer):
        at = len(started)
        copy = pltpu.make_async_remote_copy(
            src_ref=src, dst_ref=dst, send_sem=send_sem.at[at], recv_sem=recv_sem.at[at],
            device_id={axis: peer}, device_id_type=MESH)
        copy.start()
        started.append(copy)
        return copy

    def hop(src, s, at, peer):
        return pltpu.make_async_remote_copy(
            src_ref=src, dst_ref=shard(s), send_sem=hop_send.at[at], recv_sem=hop_recv.at[s],
            device_id={"feat": peer}, device_id_type=MESH)

    x_in = {d: push(x_hbm, xall.at[f], "feat", lax.rem(f + d, m)) for d in feat_d}
    own_right = hop(t_hbm, f, 0, lax.rem(f + 1, m))
    own_left = hop(t_hbm, f, 1, lax.rem(f + m - 1, m))
    pl.when(f < m - 1)(own_right.start)
    pl.when(f > 0)(own_left.start)

    steps = nearest_first(f, m)
    forwards = []

    def receive(i):
        s = steps[i]
        hop(t_hbm, s, 0, f).wait_recv()
        right = hop(shard(s), s, 2 + i, lax.rem(f + 1, m))
        left = hop(shard(s), s, 2 + i, lax.rem(f + m - 1, m))
        to_right = jnp.logical_and(s < f, f < m - 1)
        to_left = jnp.logical_and(s > f, f > 0)
        pl.when(to_right)(right.start)
        pl.when(to_left)(left.start)
        forwards.append((to_right, right))
        forwards.append((to_left, left))

    loads[5].wait()
    loads[6].wait()
    zero_tile = m * per
    order = [f] + steps
    place = []
    for s in order:
        for g in range(rb):
            for j in range(sl):
                slot = s * sl + j
                col = cols[g, slot]
                offset = lax.rem(lax.div(col, rb) - r + reach + n, n)
                live = cnt[g] > slot
                where = offset * rb + lax.rem(col, rb)
                place.append((s, g, j, (s * rb + g) * sl + j, live, where))
    inverse = {}
    for c in range((2 * reach + 1) * rb):
        for g in range(rb):
            found = jnp.int32(zero_tile)
            for _, group, _, at, live, where in place:
                if group == g:
                    found = jnp.where(jnp.logical_and(live, where == c), at, found)
            inverse[c, g] = found
    tl[zero_tile] = jnp.zeros((fb, fb), BF16)

    loads[0].wait()
    loads[1].wait()
    total = dot(xall[f], w_ref[rows_of(f), :], ((1,), (0,)))
    for d in (1, m - 1) + tuple(range(2, m - 1)):
        k = lax.rem(f + m - d, m)
        x_in[d].wait_recv()
        total = total + dot(xall[k], w_ref[rows_of(k), :], ((1,), (0,)))
    yw[pl.ds(reach * rb, rb)] = total.astype(BF16).reshape(rb, fb, fw)
    y_in = [push(yw.at[pl.ds(reach * rb, rb)], yw.at[pl.ds((reach - o) * rb, rb)], "rows",
                 lax.rem(r + o + n, n)) for o in halo]
    for i in range(m - 2):
        receive(i)
    for copy in y_in:
        copy.wait_recv()
    loads[2].wait()

    sums = [jnp.zeros((fb, fw), F32) for _ in range(rb)]
    for i in range(m):
        if i == m - 1:
            receive(i - 1)
        for s, g, j, at, live, where in place[i * per:(i + 1) * per]:
            block = yw[jnp.minimum(where, yw.shape[0] - 1)]
            product = dot(tl[at], block, ((1,), (0,)))
            sums[g] = sums[g] + jnp.where(live, product, 0.0)
    w_in = [push(w_hbm.at[rows_of(lax.rem(f + d, m))], wrow.at[f], "feat", lax.rem(f + d, m)) for d in feat_d]
    pre = jnp.concatenate(sums, axis=0)
    hidden, slope = gelu_and_slope(pre)
    loads[3].wait()
    grad_pre = (ct_ref[...].astype(F32) * slope).astype(BF16)

    def spread(o, b):
        c = (reach + o) * rb + b
        tiles = jnp.concatenate([tl[inverse[c, g]] for g in range(rb)], axis=0)
        return dot(tiles, grad_pre, ((0,), (0,)))

    s_in = {}
    far_first = list(reversed(halo))
    for b in range(rb):
        for at, o in enumerate(far_first):
            sw[b, at] = spread(o, b).astype(BF16)
            s_in[b, at] = push(sw.at[b, at], sr.at[b, at], "rows", lax.rem(r + o + n, n))
    hid_ref[...] = hidden.astype(BF16)
    saves = [pltpu.make_async_copy(src, dst, save_sem.at[i]) for i, (src, dst) in enumerate(
        ((hid_ref, hid_hbm), (gf_ref, gf_hbm), (gw_ref, gw_hbm)))]
    saves[0].start()
    grads = [spread(0, b) for b in range(rb)]
    g_in = {}
    terms = [jnp.zeros((fw, fw), F32) for _ in range(m)]
    for b in range(rb):
        grad = grads[b]
        for at in range(len(far_first)):
            s_in[b, at].wait_recv()
            grad = grad + sr[b, at].astype(F32)
        grad = grad.astype(BF16)
        gall[b, f] = grad
        for d in feat_d:
            g_in[b, d] = push(gall.at[b, f], gall.at[b, f], "feat", lax.rem(f + d, m))
        for k in range(m):
            terms[k] = terms[k] + dot(xall[k, pl.ds(b * fb, fb), :], grad, ((0,), (0,)))
    for k in range(m):
        at = pl.ds(k * fw, fw)
        gpart[at, :] = terms[k]
        gwp[at, :] = terms[k].astype(BF16)
    scale = float(rows * n) ** -0.5
    if in_sum:
        def chunk_of(d):
            return pl.ds(pl.multiple_of(lax.rem(r + n + d, n) * chunk, chunk), chunk)

        gw_in = {d: push(gwp.at[chunk_of(d)], gwr.at[d], "rows", lax.rem(r + d, n)) for d in row_d}
        part = gpart[chunk_of(0), :]
        for d in row_d:
            gw_in[d].wait_recv()
            part = part + gwr[d].astype(F32)
        own_sum = (part * scale).astype(BF16)
        gwa[0] = own_sum
        all_in = {d: push(gwa.at[0], gwa.at[d], "rows", lax.rem(r + d, n)) for d in row_d}
        gw_ref[chunk_of(0), :] = own_sum.astype(F32)
    else:
        gw_ref[...] = gpart[...] * scale

    loads[4].wait()
    for copy in w_in:
        copy.wait_recv()
    for b in range(rb):
        for d in feat_d:
            g_in[b, d].wait_recv()
        out = jnp.zeros((fb, fw), F32)
        for k in range(m):
            out = out + dot(gall[b, k], wrow[k], ((1,), (1,)))
        gf_ref[pl.ds(b * fb, fb), :] = out.astype(BF16)
    saves[1].start()
    if in_sum:
        for d in row_d:
            all_in[d].wait_recv()
            gw_ref[chunk_of(-d), :] = gwa[d].astype(F32)
    saves[2].start()
    for copy in started:
        copy.wait_send()
    pl.when(f < m - 1)(own_right.wait_send)
    pl.when(f > 0)(own_left.wait_send)
    for sent, copy in forwards:
        pl.when(sent)(copy.wait_send)
    for save in saves:
        save.wait()


def store_kernel(a, b, c, a_out, b_out, c_out, sem):
    copies = [pltpu.make_async_copy(src, dst, sem.at[i])
              for i, (src, dst) in enumerate(((c, c_out), (a, a_out), (b, b_out)))]
    for copy in copies:
        copy.start()
    for copy in copies:
        copy.wait()


def on_device(features, weight, block_values, columns, counts, cotangent):
    n = lax.axis_size("rows")
    m = lax.axis_size("feat")
    reach = min(4, (n - 1) // 3)
    rb, sl, fb, _ = block_values.shape
    rows, fw = features.shape
    depth = weight.shape[0]
    in_sum = depth % (n * 16) == 0
    chunk = depth // n if in_sum else 16
    span = 2 * reach + 1
    copies = (2 + rb) * (m - 1) + (1 + rb) * 2 * reach + (2 * (n - 1) if in_sum else 0)
    hbm = pl.BlockSpec(memory_space=pltpu.HBM)
    hidden, grad_features, grad_weight = pl.pallas_call(
        functools.partial(kernel, n, m, reach, rb, sl, in_sum),
        out_shape=(
            jax.ShapeDtypeStruct((rows, fw), BF16),
            jax.ShapeDtypeStruct((rows, fw), BF16),
            jax.ShapeDtypeStruct((depth, fw), F32),
        ),
        in_specs=[hbm, hbm, hbm, hbm, hbm, hbm],
        out_specs=(hbm, hbm, hbm),
        scratch_shapes=[
            pltpu.VMEM((rows, fw), BF16),
            pltpu.VMEM((rows, fw), BF16),
            pltpu.VMEM((depth, fw), F32),
            pltpu.VMEM((m, rows, fw), BF16),
            pltpu.VMEM((depth, fw), BF16),
            pltpu.VMEM((rows, fw), BF16),
            pltpu.VMEM((m, fw, fw), BF16),
            pltpu.VMEM((m * rb * sl + 1, fb, fb), BF16),
            pltpu.VMEM((span * rb, fb, fw), BF16),
            pltpu.VMEM((rb, 2 * reach, fb, fw), BF16),
            pltpu.VMEM((rb, 2 * reach, fb, fw), BF16),
            pltpu.VMEM((rb, m, fb, fw), BF16),
            pltpu.VMEM((depth, fw), F32),
            pltpu.VMEM((depth, fw), BF16),
            pltpu.VMEM((n if in_sum else 1, chunk, fw), BF16),
            pltpu.VMEM((n if in_sum else 1, chunk, fw), BF16),
            pltpu.SemaphoreType.DMA((copies,)),
            pltpu.SemaphoreType.DMA((copies,)),
            pltpu.SemaphoreType.DMA((m + 1,)),
            pltpu.SemaphoreType.DMA((m,)),
            pltpu.SemaphoreType.DMA((7,)),
            pltpu.SemaphoreType.DMA((3,)),
            pltpu.SMEM(columns.shape, jnp.int32),
            pltpu.SMEM(counts.shape, jnp.int32),
        ],
        compiler_params=pltpu.CompilerParams(
            collective_id=0, has_side_effects=True, vmem_limit_bytes=56 * 1024 * 1024),
    )(columns, counts, features, weight, block_values.reshape(rb * sl, fb, fb), cotangent)
    if not in_sum:
        grad_weight = lax.psum(grad_weight, "rows")
    results = (hidden, grad_features, grad_weight)
    return pl.pallas_call(
        store_kernel,
        out_shape=tuple(jax.ShapeDtypeStruct(v.shape, v.dtype) for v in results),
        in_specs=[hbm] * 3,
        out_specs=(hbm,) * 3,
        scratch_shapes=[pltpu.SemaphoreType.DMA((3,))],
        compiler_params=pltpu.CompilerParams(vmem_limit_bytes=56 * 1024 * 1024),
    )(*results)


def solution(mesh):
    in_specs = (
        P("rows", "feat"),
        P(None, "feat"),
        P("rows", "feat", None, None),
        P("rows", None),
        P("rows"),
        P("rows", "feat"),
    )
    out_specs = (P("rows", "feat"), P("rows", "feat"), P(None, "feat"))
    return jax.shard_map(
        on_device, mesh=mesh, in_specs=in_specs, out_specs=out_specs, check_vma=False
    )
```

```python
import functools

import jax
import jax.numpy as jnp
from jax import lax
from jax.experimental import pallas as pl
from jax.experimental.pallas import tpu as pltpu
from jax.sharding import PartitionSpec as P

MESH = pl.DeviceIdType.MESH
F32 = jnp.float32
BF16 = jnp.bfloat16
GELU_SCALE = 0.7978845608028654
GELU_CUBE = 0.044715


def gelu_and_slope(v):
    square = v * v
    t = jnp.tanh(GELU_SCALE * (v + GELU_CUBE * (square * v)))
    half = 0.5 * (1.0 + t)
    inner = GELU_SCALE * (1.0 + 3.0 * GELU_CUBE * square)
    return v * half, half + 0.5 * v * (1.0 - t * t) * inner


def dot(a, b, contract):
    return lax.dot_general(a, b, (contract, ((), ())), preferred_element_type=F32)


def nearest_first(f, m):
    tables = []
    for me in range(m):
        line = [p for e in range(1, m) for p in (me - e, me + e) if 0 <= p < m]
        tables.append(line)
    steps = []
    for i in range(m - 1):
        at = jnp.int32(tables[0][i])
        for me in range(1, m):
            at = jnp.where(f == me, tables[me][i], at)
        steps.append(at)
    return steps


def kernel(n, m, reach, rb, sl, in_sum, cols_hbm, cnt_hbm, x_hbm, w_hbm, t_hbm, ct_hbm,
           hid_ref, gf_ref, gw_ref, xall, w_ref, ct_ref, wrow, tl, yw, sw, sr, gall, gpart, gwp, gwr, gwa,
           send_sem, recv_sem, hop_send, hop_recv, load_sem, cols, cnt):
    r = lax.axis_index("rows")
    f = lax.axis_index("feat")
    fb = t_hbm.shape[1]
    rows, fw = x_hbm.shape
    per = rb * sl
    chunk = gwr.shape[1]
    halo = [o for d in range(1, reach + 1) for o in (d, -d)]
    feat_d = list(range(1, m))
    row_d = list(range(1, n)) if in_sum else []
    row_peers = [d % n for d in (row_d if in_sum else halo)]

    def shard(s):
        return tl.at[pl.ds(s * per, per)]

    def rows_of(s):
        return pl.ds(pl.multiple_of(s * fw, fw), fw)

    loads = [
        pltpu.make_async_copy(x_hbm, xall.at[f], load_sem.at[0]),
        pltpu.make_async_copy(w_hbm, w_ref, load_sem.at[1]),
        pltpu.make_async_copy(t_hbm, shard(f), load_sem.at[2]),
        pltpu.make_async_copy(ct_hbm, ct_ref, load_sem.at[3]),
        pltpu.make_async_copy(w_hbm.at[rows_of(f)], wrow.at[f], load_sem.at[4]),
        pltpu.make_async_copy(cols_hbm, cols, load_sem.at[5]),
        pltpu.make_async_copy(cnt_hbm, cnt, load_sem.at[6]),
    ]
    for load in loads:
        load.start()

    barrier = pltpu.get_barrier_semaphore()
    for d in feat_d:
        pl.semaphore_signal(barrier, inc=1, device_id={"feat": lax.rem(f + d, m)}, device_id_type=MESH)
    for d in row_peers:
        pl.semaphore_signal(barrier, inc=1, device_id={"rows": lax.rem(r + d, n)}, device_id_type=MESH)
    pl.semaphore_wait(barrier, len(feat_d) + len(row_peers))

    started = []

    def push(src, dst, axis, peer):
        at = len(started)
        copy = pltpu.make_async_remote_copy(
            src_ref=src, dst_ref=dst, send_sem=send_sem.at[at], recv_sem=recv_sem.at[at],
            device_id={axis: peer}, device_id_type=MESH)
        copy.start()
        started.append(copy)
        return copy

    def hop(src, s, at, peer):
        return pltpu.make_async_remote_copy(
            src_ref=src, dst_ref=shard(s), send_sem=hop_send.at[at], recv_sem=hop_recv.at[s],
            device_id={"feat": peer}, device_id_type=MESH)

    x_in = {d: push(x_hbm, xall.at[f], "feat", lax.rem(f + d, m)) for d in feat_d}
    own_right = hop(t_hbm, f, 0, lax.rem(f + 1, m))
    own_left = hop(t_hbm, f, 1, lax.rem(f + m - 1, m))
    pl.when(f < m - 1)(own_right.start)
    pl.when(f > 0)(own_left.start)

    steps = nearest_first(f, m)
    forwards = []

    def receive(i):
        s = steps[i]
        hop(t_hbm, s, 0, f).wait_recv()
        right = hop(shard(s), s, 2 + i, lax.rem(f + 1, m))
        left = hop(shard(s), s, 2 + i, lax.rem(f + m - 1, m))
        to_right = jnp.logical_and(s < f, f < m - 1)
        to_left = jnp.logical_and(s > f, f > 0)
        pl.when(to_right)(right.start)
        pl.when(to_left)(left.start)
        forwards.append((to_right, right))
        forwards.append((to_left, left))

    loads[5].wait()
    loads[6].wait()
    zero_tile = m * per
    order = [f] + steps
    place = []
    for s in order:
        for g in range(rb):
            for j in range(sl):
                slot = s * sl + j
                col = cols[g, slot]
                offset = lax.rem(lax.div(col, rb) - r + reach + n, n)
                live = cnt[g] > slot
                where = offset * rb + lax.rem(col, rb)
                place.append((s, g, j, (s * rb + g) * sl + j, live, where))
    inverse = {}
    for c in range((2 * reach + 1) * rb):
        for g in range(rb):
            found = jnp.int32(zero_tile)
            for _, group, _, at, live, where in place:
                if group == g:
                    found = jnp.where(jnp.logical_and(live, where == c), at, found)
            inverse[c, g] = found
    tl[zero_tile] = jnp.zeros((fb, fb), BF16)

    loads[0].wait()
    loads[1].wait()
    total = dot(xall[f], w_ref[rows_of(f), :], ((1,), (0,)))
    for d in (1, m - 1) + tuple(range(2, m - 1)):
        k = lax.rem(f + m - d, m)
        x_in[d].wait_recv()
        total = total + dot(xall[k], w_ref[rows_of(k), :], ((1,), (0,)))
    yw[pl.ds(reach * rb, rb)] = total.astype(BF16).reshape(rb, fb, fw)
    y_in = [push(yw.at[pl.ds(reach * rb, rb)], yw.at[pl.ds((reach - o) * rb, rb)], "rows",
                 lax.rem(r + o + n, n)) for o in halo]
    for i in range(m - 2):
        receive(i)
    for copy in y_in:
        copy.wait_recv()
    loads[2].wait()

    sums = [jnp.zeros((fb, fw), F32) for _ in range(rb)]
    for i in range(m):
        if i == m - 1:
            receive(i - 1)
        for s, g, j, at, live, where in place[i * per:(i + 1) * per]:
            block = yw[jnp.minimum(where, yw.shape[0] - 1)]
            product = dot(tl[at], block, ((1,), (0,)))
            sums[g] = sums[g] + jnp.where(live, product, 0.0)
    w_in = [push(w_hbm.at[rows_of(lax.rem(f + d, m))], wrow.at[f], "feat", lax.rem(f + d, m)) for d in feat_d]
    pre = jnp.concatenate(sums, axis=0)
    hidden, slope = gelu_and_slope(pre)
    loads[3].wait()
    grad_pre = (ct_ref[...].astype(F32) * slope).astype(BF16)

    def spread(o, b):
        c = (reach + o) * rb + b
        tiles = jnp.concatenate([tl[inverse[c, g]] for g in range(rb)], axis=0)
        return dot(tiles, grad_pre, ((0,), (0,)))

    s_in = {}
    far_first = list(reversed(halo))
    for b in range(rb):
        for at, o in enumerate(far_first):
            sw[b, at] = spread(o, b).astype(BF16)
            s_in[b, at] = push(sw.at[b, at], sr.at[b, at], "rows", lax.rem(r + o + n, n))
    hid_ref[...] = hidden.astype(BF16)
    grads = [spread(0, b) for b in range(rb)]
    g_in = {}
    terms = [jnp.zeros((fw, fw), F32) for _ in range(m)]
    for b in range(rb):
        grad = grads[b]
        for at in range(len(far_first)):
            s_in[b, at].wait_recv()
            grad = grad + sr[b, at].astype(F32)
        grad = grad.astype(BF16)
        gall[b, f] = grad
        for d in feat_d:
            g_in[b, d] = push(gall.at[b, f], gall.at[b, f], "feat", lax.rem(f + d, m))
        for k in range(m):
            terms[k] = terms[k] + dot(xall[k, pl.ds(b * fb, fb), :], grad, ((0,), (0,)))
    for k in range(m):
        at = pl.ds(k * fw, fw)
        gpart[at, :] = terms[k]
        gwp[at, :] = terms[k].astype(BF16)
    scale = float(rows * n) ** -0.5
    if in_sum:
        def chunk_of(d):
            return pl.ds(pl.multiple_of(lax.rem(r + n + d, n) * chunk, chunk), chunk)

        gw_in = {d: push(gwp.at[chunk_of(d)], gwr.at[d], "rows", lax.rem(r + d, n)) for d in row_d}
        part = gpart[chunk_of(0), :]
        for d in row_d:
            gw_in[d].wait_recv()
            part = part + gwr[d].astype(F32)
        own_sum = (part * scale).astype(BF16)
        gwa[0] = own_sum
        all_in = {d: push(gwa.at[0], gwa.at[d], "rows", lax.rem(r + d, n)) for d in row_d}
        gw_ref[chunk_of(0), :] = own_sum.astype(F32)
    else:
        gw_ref[...] = gpart[...] * scale

    loads[4].wait()
    for copy in w_in:
        copy.wait_recv()
    for b in range(rb):
        for d in feat_d:
            g_in[b, d].wait_recv()
        out = jnp.zeros((fb, fw), F32)
        for k in range(m):
            out = out + dot(gall[b, k], wrow[k], ((1,), (1,)))
        gf_ref[pl.ds(b * fb, fb), :] = out.astype(BF16)
    if in_sum:
        for d in row_d:
            all_in[d].wait_recv()
            gw_ref[chunk_of(-d), :] = gwa[d].astype(F32)
    for copy in started:
        copy.wait_send()
    pl.when(f < m - 1)(own_right.wait_send)
    pl.when(f > 0)(own_left.wait_send)
    for sent, copy in forwards:
        pl.when(sent)(copy.wait_send)


def store_kernel(a, b, c, a_out, b_out, c_out, sem):
    copies = [pltpu.make_async_copy(src, dst, sem.at[i])
              for i, (src, dst) in enumerate(((c, c_out), (a, a_out), (b, b_out)))]
    for copy in copies:
        copy.start()
    for copy in copies:
        copy.wait()


def on_device(features, weight, block_values, columns, counts, cotangent):
    n = lax.axis_size("rows")
    m = lax.axis_size("feat")
    reach = min(4, (n - 1) // 3)
    rb, sl, fb, _ = block_values.shape
    rows, fw = features.shape
    depth = weight.shape[0]
    in_sum = depth % (n * 16) == 0
    chunk = depth // n if in_sum else 16
    span = 2 * reach + 1
    copies = (2 + rb) * (m - 1) + (1 + rb) * 2 * reach + (2 * (n - 1) if in_sum else 0)
    vmem = pl.BlockSpec(memory_space=pltpu.VMEM)
    hbm = pl.BlockSpec(memory_space=pltpu.HBM)
    hidden, grad_features, grad_weight = pl.pallas_call(
        functools.partial(kernel, n, m, reach, rb, sl, in_sum),
        out_shape=(
            pltpu.VMEM((rows, fw), BF16),
            pltpu.VMEM((rows, fw), BF16),
            pltpu.VMEM((depth, fw), F32),
        ),
        in_specs=[hbm, hbm, hbm, hbm, hbm, hbm],
        out_specs=(vmem, vmem, vmem),
        scratch_shapes=[
            pltpu.VMEM((m, rows, fw), BF16),
            pltpu.VMEM((depth, fw), BF16),
            pltpu.VMEM((rows, fw), BF16),
            pltpu.VMEM((m, fw, fw), BF16),
            pltpu.VMEM((m * rb * sl + 1, fb, fb), BF16),
            pltpu.VMEM((span * rb, fb, fw), BF16),
            pltpu.VMEM((rb, 2 * reach, fb, fw), BF16),
            pltpu.VMEM((rb, 2 * reach, fb, fw), BF16),
            pltpu.VMEM((rb, m, fb, fw), BF16),
            pltpu.VMEM((depth, fw), F32),
            pltpu.VMEM((depth, fw), BF16),
            pltpu.VMEM((n if in_sum else 1, chunk, fw), BF16),
            pltpu.VMEM((n if in_sum else 1, chunk, fw), BF16),
            pltpu.SemaphoreType.DMA((copies,)),
            pltpu.SemaphoreType.DMA((copies,)),
            pltpu.SemaphoreType.DMA((m + 1,)),
            pltpu.SemaphoreType.DMA((m,)),
            pltpu.SemaphoreType.DMA((7,)),
            pltpu.SMEM(columns.shape, jnp.int32),
            pltpu.SMEM(counts.shape, jnp.int32),
        ],
        compiler_params=pltpu.CompilerParams(
            collective_id=0, has_side_effects=True, vmem_limit_bytes=32 * 1024 * 1024),
    )(*(pltpu.with_memory_space_constraint(v, pltpu.HBM) for v in (
        columns, counts, features, weight, block_values.reshape(rb * sl, fb, fb), cotangent)))
    if not in_sum:
        grad_weight = lax.psum(grad_weight, "rows")
    results = (hidden, grad_features, grad_weight)
    return pl.pallas_call(
        store_kernel,
        out_shape=tuple(jax.ShapeDtypeStruct(v.shape, v.dtype) for v in results),
        in_specs=[vmem] * 3,
        out_specs=(hbm,) * 3,
        scratch_shapes=[pltpu.SemaphoreType.DMA((3,))],
        compiler_params=pltpu.CompilerParams(vmem_limit_bytes=32 * 1024 * 1024),
    )(*results)


def solution(mesh):
    in_specs = (
        P("rows", "feat"),
        P(None, "feat"),
        P("rows", "feat", None, None),
        P("rows", None),
        P("rows"),
        P("rows", "feat"),
    )
    out_specs = (P("rows", "feat"), P("rows", "feat"), P(None, "feat"))
    return jax.shard_map(
        on_device, mesh=mesh, in_specs=in_specs, out_specs=out_specs, check_vma=False
    )
```

```python
import functools

import jax
import jax.numpy as jnp
from jax import lax
from jax.experimental import pallas as pl
from jax.experimental.pallas import tpu as pltpu
from jax.sharding import PartitionSpec as P

MESH = pl.DeviceIdType.MESH
F32 = jnp.float32
BF16 = jnp.bfloat16
GELU_SCALE = 0.7978845608028654
GELU_CUBE = 0.044715


def gelu_and_slope(v):
    square = v * v
    t = jnp.tanh(GELU_SCALE * (v + GELU_CUBE * (square * v)))
    half = 0.5 * (1.0 + t)
    inner = GELU_SCALE * (1.0 + 3.0 * GELU_CUBE * square)
    return v * half, half + 0.5 * v * (1.0 - t * t) * inner


def dot(a, b, contract):
    return lax.dot_general(a, b, (contract, ((), ())), preferred_element_type=F32)


def nearest_first(f, m):
    tables = []
    for me in range(m):
        line = [p for e in range(1, m) for p in (me - e, me + e) if 0 <= p < m]
        tables.append(line)
    steps = []
    for i in range(m - 1):
        at = jnp.int32(tables[0][i])
        for me in range(1, m):
            at = jnp.where(f == me, tables[me][i], at)
        steps.append(at)
    return steps


def kernel(n, m, reach, rb, sl, in_sum, cols_hbm, cnt_hbm, x_hbm, w_hbm, t_hbm, ct_hbm,
           hid_ref, gf_ref, gw_ref, xall, w_ref, ct_ref, wrow, tl, tl_t, x_t, yw, sw, sr, gall, gpart, gwp, gwr, gwa,
           send_sem, recv_sem, hop_send, hop_recv, load_sem, cols, cnt):

    r = lax.axis_index("rows")
    f = lax.axis_index("feat")
    fb = t_hbm.shape[1]
    rows, fw = x_hbm.shape
    per = rb * sl
    chunk = gwr.shape[1]
    halo = [o for d in range(1, reach + 1) for o in (d, -d)]
    feat_d = list(range(1, m))
    row_d = list(range(1, n)) if in_sum else []
    row_peers = [d % n for d in (row_d if in_sum else halo)]

    def shard(s):
        return tl.at[pl.ds(s * per, per)]

    def rows_of(s):
        return pl.ds(pl.multiple_of(s * fw, fw), fw)

    loads = [
        pltpu.make_async_copy(x_hbm, xall.at[f], load_sem.at[0]),
        pltpu.make_async_copy(w_hbm, w_ref, load_sem.at[1]),
        pltpu.make_async_copy(t_hbm, shard(f), load_sem.at[2]),
        pltpu.make_async_copy(ct_hbm, ct_ref, load_sem.at[3]),
        pltpu.make_async_copy(w_hbm.at[rows_of(f)], wrow.at[f], load_sem.at[4]),
        pltpu.make_async_copy(cols_hbm, cols, load_sem.at[5]),
        pltpu.make_async_copy(cnt_hbm, cnt, load_sem.at[6]),
    ]
    for load in loads:
        load.start()

    barrier = pltpu.get_barrier_semaphore()
    for d in feat_d:
        pl.semaphore_signal(barrier, inc=1, device_id={"feat": lax.rem(f + d, m)}, device_id_type=MESH)
    for d in row_peers:
        pl.semaphore_signal(barrier, inc=1, device_id={"rows": lax.rem(r + d, n)}, device_id_type=MESH)
    pl.semaphore_wait(barrier, len(feat_d) + len(row_peers))

    started = []

    def push(src, dst, axis, peer):
        at = len(started)
        copy = pltpu.make_async_remote_copy(
            src_ref=src, dst_ref=dst, send_sem=send_sem.at[at], recv_sem=recv_sem.at[at],
            device_id={axis: peer}, device_id_type=MESH)
        copy.start()
        started.append(copy)
        return copy

    def slot_of(kind, s):
        return shard(s) if kind else xall.at[s]

    def hop(kind, src, s, at, peer):
        return pltpu.make_async_remote_copy(
            src_ref=src, dst_ref=slot_of(kind, s), send_sem=hop_send.at[kind, at],
            recv_sem=hop_recv.at[kind, s], device_id={"feat": peer}, device_id_type=MESH)

    forwards = []

    def onward(kind, src, s, at, to_right, to_left):
        right = hop(kind, src, s, at, lax.rem(f + 1, m))
        left = hop(kind, src, s, at + 1, lax.rem(f + m - 1, m))
        pl.when(to_right)(right.start)
        pl.when(to_left)(left.start)
        forwards.append((to_right, right))
        forwards.append((to_left, left))

    for kind, src in enumerate((x_hbm, t_hbm)):
        onward(kind, src, f, 0, f < m - 1, f > 0)
    steps = nearest_first(f, m)

    def receive(kind, i):
        s = steps[i]
        hop(kind, slot_of(kind, s), s, 0, lax.rem(f + 1, m)).wait_recv()
        onward(kind, slot_of(kind, s), s, 2 + 2 * i, jnp.logical_and(s < f, f < m - 1),
               jnp.logical_and(s > f, f > 0))

    loads[5].wait()
    loads[6].wait()
    zero_tile = m * per
    order = [f] + steps
    place = []
    for s in order:
        for g in range(rb):
            for j in range(sl):
                slot = s * sl + j
                col = cols[g, slot]
                offset = lax.rem(lax.div(col, rb) - r + reach + n, n)
                live = cnt[g] > slot
                where = offset * rb + lax.rem(col, rb)
                place.append((s, g, j, (s * rb + g) * sl + j, live, where))
    inverse = {}
    for c in range((2 * reach + 1) * rb):
        for g in range(rb):
            found = jnp.int32(zero_tile)
            for _, group, _, at, live, where in place:
                if group == g:
                    found = jnp.where(jnp.logical_and(live, where == c), at, found)
            inverse[c, g] = found
    tl_t[zero_tile] = jnp.zeros((fb, fb), BF16)

    loads[0].wait()
    loads[1].wait()
    total = dot(xall[f], w_ref[rows_of(f), :], ((1,), (0,)))
    for i, k in enumerate(steps):
        receive(0, i)
        total = total + dot(xall[k], w_ref[rows_of(k), :], ((1,), (0,)))
    yw[pl.ds(reach * rb, rb)] = total.astype(BF16).reshape(rb, fb, fw)
    y_in = [push(yw.at[pl.ds(reach * rb, rb)], yw.at[pl.ds((reach - o) * rb, rb)], "rows",
                 lax.rem(r + o + n, n)) for o in halo]
    for k in range(m):
        x_t[k] = xall[k].T
    for i in range(m - 2):
        receive(1, i)
    for copy in y_in:
        copy.wait_recv()
    loads[2].wait()

    sums = [jnp.zeros((fb, fw), F32) for _ in range(rb)]
    for i in range(m):
        if i == m - 1:
            receive(1, i - 1)
        for s, g, j, at, live, where in place[i * per:(i + 1) * per]:
            block = yw[jnp.minimum(where, yw.shape[0] - 1)]
            product = dot(tl[at], block, ((1,), (0,)))
            sums[g] = sums[g] + jnp.where(live, product, 0.0)
            tl_t[at] = tl[at].T
    w_in = [push(w_hbm.at[rows_of(lax.rem(f + d, m))], wrow.at[f], "feat", lax.rem(f + d, m)) for d in feat_d]
    pre = jnp.concatenate(sums, axis=0)
    hidden, slope = gelu_and_slope(pre)
    loads[3].wait()
    grad_pre = (ct_ref[...].astype(F32) * slope).astype(BF16)

    def spread(o, b):
        c = (reach + o) * rb + b
        tiles = jnp.concatenate([tl_t[inverse[c, g]] for g in range(rb)], axis=1)
        return dot(tiles, grad_pre, ((1,), (0,)))

    s_in = {}
    far_first = list(reversed(halo))
    for b in range(rb):
        for at, o in enumerate(far_first):
            sw[b, at] = spread(o, b).astype(BF16)
            s_in[b, at] = push(sw.at[b, at], sr.at[b, at], "rows", lax.rem(r + o + n, n))
    hid_ref[...] = hidden.astype(BF16)
    grads = [spread(0, b) for b in range(rb)]
    g_in = {}
    terms = [jnp.zeros((fw, fw), F32) for _ in range(m)]
    for b in range(rb):
        grad = grads[b]
        for at in range(len(far_first)):
            s_in[b, at].wait_recv()
            grad = grad + sr[b, at].astype(F32)
        grad = grad.astype(BF16)
        gall[b, f] = grad
        for d in feat_d:
            g_in[b, d] = push(gall.at[b, f], gall.at[b, f], "feat", lax.rem(f + d, m))
        for k in range(m):
            terms[k] = terms[k] + dot(x_t[k, :, pl.ds(b * fb, fb)], grad, ((1,), (0,)))
    for k in range(m):
        at = pl.ds(k * fw, fw)
        gpart[at, :] = terms[k]
        gwp[at, :] = terms[k].astype(BF16)
    scale = float(rows * n) ** -0.5
    if in_sum:
        def chunk_of(d):
            return pl.ds(pl.multiple_of(lax.rem(r + n + d, n) * chunk, chunk), chunk)

        gw_in = {d: push(gwp.at[chunk_of(d)], gwr.at[d], "rows", lax.rem(r + d, n)) for d in row_d}
        part = gpart[chunk_of(0), :]
        for d in row_d:
            gw_in[d].wait_recv()
            part = part + gwr[d].astype(F32)
        own_sum = (part * scale).astype(BF16)
        gwa[0] = own_sum
        all_in = {d: push(gwa.at[0], gwa.at[d], "rows", lax.rem(r + d, n)) for d in row_d}
        gw_ref[chunk_of(0), :] = own_sum.astype(F32)
    else:
        gw_ref[...] = gpart[...] * scale

    loads[4].wait()
    for copy in w_in:
        copy.wait_recv()
    for b in range(rb):
        for d in feat_d:
            g_in[b, d].wait_recv()
        out = jnp.zeros((fb, fw), F32)
        for k in range(m):
            out = out + dot(gall[b, k], wrow[k], ((1,), (1,)))
        gf_ref[pl.ds(b * fb, fb), :] = out.astype(BF16)
    if in_sum:
        for d in row_d:
            all_in[d].wait_recv()
            gw_ref[chunk_of(-d), :] = gwa[d].astype(F32)
    for copy in started:
        copy.wait_send()
    for sent, copy in forwards:
        pl.when(sent)(copy.wait_send)


def store_kernel(a, b, c, a_out, b_out, c_out, sem):
    copies = [pltpu.make_async_copy(src, dst, sem.at[i])
              for i, (src, dst) in enumerate(((c, c_out), (a, a_out), (b, b_out)))]
    for copy in copies:
        copy.start()
    for copy in copies:
        copy.wait()


def on_device(features, weight, block_values, columns, counts, cotangent):
    n = lax.axis_size("rows")
    m = lax.axis_size("feat")
    reach = min(4, (n - 1) // 3)
    rb, sl, fb, _ = block_values.shape
    rows, fw = features.shape
    depth = weight.shape[0]
    in_sum = depth % (n * 16) == 0
    chunk = depth // n if in_sum else 16
    span = 2 * reach + 1
    copies = (1 + rb) * (m - 1) + (1 + rb) * 2 * reach + (2 * (n - 1) if in_sum else 0)
    vmem = pl.BlockSpec(memory_space=pltpu.VMEM)
    hbm = pl.BlockSpec(memory_space=pltpu.HBM)
    hidden, grad_features, grad_weight = pl.pallas_call(
        functools.partial(kernel, n, m, reach, rb, sl, in_sum),
        out_shape=(
            pltpu.VMEM((rows, fw), BF16),
            pltpu.VMEM((rows, fw), BF16),
            pltpu.VMEM((depth, fw), F32),
        ),
        in_specs=[hbm, hbm, hbm, hbm, hbm, hbm],
        out_specs=(vmem, vmem, vmem),
        scratch_shapes=[
            pltpu.VMEM((m, rows, fw), BF16),
            pltpu.VMEM((depth, fw), BF16),
            pltpu.VMEM((rows, fw), BF16),
            pltpu.VMEM((m, fw, fw), BF16),
            pltpu.VMEM((m * rb * sl, fb, fb), BF16),
            pltpu.VMEM((m * rb * sl + 1, fb, fb), BF16),
            pltpu.VMEM((m, fw, rows), BF16),
            pltpu.VMEM((span * rb, fb, fw), BF16),
            pltpu.VMEM((rb, 2 * reach, fb, fw), BF16),
            pltpu.VMEM((rb, 2 * reach, fb, fw), BF16),
            pltpu.VMEM((rb, m, fb, fw), BF16),
            pltpu.VMEM((depth, fw), F32),
            pltpu.VMEM((depth, fw), BF16),
            pltpu.VMEM((n if in_sum else 1, chunk, fw), BF16),
            pltpu.VMEM((n if in_sum else 1, chunk, fw), BF16),
            pltpu.SemaphoreType.DMA((copies,)),
            pltpu.SemaphoreType.DMA((copies,)),
            pltpu.SemaphoreType.DMA((2, 2 * m)),
            pltpu.SemaphoreType.DMA((2, m)),
            pltpu.SemaphoreType.DMA((7,)),
            pltpu.SMEM(columns.shape, jnp.int32),
            pltpu.SMEM(counts.shape, jnp.int32),
        ],
        compiler_params=pltpu.CompilerParams(
            collective_id=0, has_side_effects=True, vmem_limit_bytes=32 * 1024 * 1024),
    )(*(pltpu.with_memory_space_constraint(v, pltpu.HBM) for v in (
        columns, counts, features, weight, block_values.reshape(rb * sl, fb, fb), cotangent)))
    if not in_sum:
        grad_weight = lax.psum(grad_weight, "rows")
    results = (hidden, grad_features, grad_weight)
    return pl.pallas_call(
        store_kernel,
        out_shape=tuple(jax.ShapeDtypeStruct(v.shape, v.dtype) for v in results),
        in_specs=[vmem] * 3,
        out_specs=(hbm,) * 3,
        scratch_shapes=[pltpu.SemaphoreType.DMA((3,))],
        compiler_params=pltpu.CompilerParams(vmem_limit_bytes=32 * 1024 * 1024),
    )(*results)


def solution(mesh):
    in_specs = (
        P("rows", "feat"),
        P(None, "feat"),
        P("rows", "feat", None, None),
        P("rows", None),
        P("rows"),
        P("rows", "feat"),
    )
    out_specs = (P("rows", "feat"), P("rows", "feat"), P(None, "feat"))
    return jax.shard_map(
        on_device, mesh=mesh, in_specs=in_specs, out_specs=out_specs, check_vma=False
    )
```

```python
import functools

import jax
import jax.numpy as jnp
from jax import lax
from jax.experimental import pallas as pl
from jax.experimental.pallas import tpu as pltpu
from jax.sharding import PartitionSpec as P

MESH = pl.DeviceIdType.MESH
F32 = jnp.float32
BF16 = jnp.bfloat16
GELU_SCALE = 0.7978845608028654
GELU_CUBE = 0.044715


def gelu_and_slope(v):
    square = v * v
    t = jnp.tanh(GELU_SCALE * (v + GELU_CUBE * (square * v)))
    half = 0.5 * (1.0 + t)
    inner = GELU_SCALE * (1.0 + 3.0 * GELU_CUBE * square)
    return v * half, half + 0.5 * v * (1.0 - t * t) * inner


def dot(a, b, contract):
    return lax.dot_general(a, b, (contract, ((), ())), preferred_element_type=F32)


def nearest_first(f, m):
    tables = []
    for me in range(m):
        line = [p for e in range(1, m) for p in (me - e, me + e) if 0 <= p < m]
        tables.append(line)
    steps = []
    for i in range(m - 1):
        at = jnp.int32(tables[0][i])
        for me in range(1, m):
            at = jnp.where(f == me, tables[me][i], at)
        steps.append(at)
    return steps


def kernel(n, m, reach, rb, sl, in_sum, cols_hbm, cnt_hbm, x_hbm, w_hbm, t_hbm, ct_hbm,
           hid_ref, gf_ref, gw_ref, xall, w_ref, ct_ref, wrow, w_t, tl, tl_t, x_t, yw, sw, sr, gall, gpart, gwp, gwr, gwa,
           send_sem, recv_sem, hop_send, hop_recv, load_sem, cols, cnt):

    r = lax.axis_index("rows")
    f = lax.axis_index("feat")
    fb = t_hbm.shape[1]
    rows, fw = x_hbm.shape
    per = rb * sl
    chunk = gwr.shape[1]
    halo = [o for d in range(1, reach + 1) for o in (d, -d)]
    feat_d = list(range(1, m))
    row_d = list(range(1, n)) if in_sum else []
    row_peers = [d % n for d in (row_d if in_sum else halo)]

    def shard(s):
        return tl.at[pl.ds(s * per, per)]

    def rows_of(s):
        return pl.ds(pl.multiple_of(s * fw, fw), fw)

    loads = [
        pltpu.make_async_copy(x_hbm, xall.at[f], load_sem.at[0]),
        pltpu.make_async_copy(w_hbm, w_ref, load_sem.at[1]),
        pltpu.make_async_copy(t_hbm, shard(f), load_sem.at[2]),
        pltpu.make_async_copy(ct_hbm, ct_ref, load_sem.at[3]),
        pltpu.make_async_copy(w_hbm.at[rows_of(f)], wrow.at[f], load_sem.at[4]),
        pltpu.make_async_copy(cols_hbm, cols, load_sem.at[5]),
        pltpu.make_async_copy(cnt_hbm, cnt, load_sem.at[6]),
    ]
    for load in loads:
        load.start()

    barrier = pltpu.get_barrier_semaphore()
    for d in feat_d:
        pl.semaphore_signal(barrier, inc=1, device_id={"feat": lax.rem(f + d, m)}, device_id_type=MESH)
    for d in row_peers:
        pl.semaphore_signal(barrier, inc=1, device_id={"rows": lax.rem(r + d, n)}, device_id_type=MESH)
    pl.semaphore_wait(barrier, len(feat_d) + len(row_peers))

    started = []

    def push(src, dst, axis, peer):
        at = len(started)
        copy = pltpu.make_async_remote_copy(
            src_ref=src, dst_ref=dst, send_sem=send_sem.at[at], recv_sem=recv_sem.at[at],
            device_id={axis: peer}, device_id_type=MESH)
        copy.start()
        started.append(copy)
        return copy

    def slot_of(kind, s):
        return tl.at[pl.ds((s * rb + kind - 1) * sl, sl)] if kind else xall.at[s]

    def hop(kind, src, s, at, peer):
        return pltpu.make_async_remote_copy(
            src_ref=src, dst_ref=slot_of(kind, s), send_sem=hop_send.at[kind, at],
            recv_sem=hop_recv.at[kind, s], device_id={"feat": peer}, device_id_type=MESH)

    forwards = []

    def onward(kind, src, s, at, to_right, to_left):
        right = hop(kind, src, s, at, lax.rem(f + 1, m))
        left = hop(kind, src, s, at + 1, lax.rem(f + m - 1, m))
        pl.when(to_right)(right.start)
        pl.when(to_left)(left.start)
        forwards.append((to_right, right))
        forwards.append((to_left, left))

    for kind, src in enumerate([x_hbm] + [t_hbm.at[pl.ds(g * sl, sl)] for g in range(rb)]):
        onward(kind, src, f, 0, f < m - 1, f > 0)
    steps = nearest_first(f, m)

    def receive(kind, i):
        s = steps[i]
        hop(kind, slot_of(kind, s), s, 0, lax.rem(f + 1, m)).wait_recv()
        onward(kind, slot_of(kind, s), s, 2 + 2 * i, jnp.logical_and(s < f, f < m - 1),
               jnp.logical_and(s > f, f > 0))

    loads[5].wait()
    loads[6].wait()
    zero_tile = m * per
    order = [f] + steps
    place = []
    for s in order:
        for g in range(rb):
            for j in range(sl):
                slot = s * sl + j
                col = cols[g, slot]
                offset = lax.rem(lax.div(col, rb) - r + reach + n, n)
                live = cnt[g] > slot
                where = offset * rb + lax.rem(col, rb)
                place.append((s, g, j, (s * rb + g) * sl + j, live, where))
    inverse = {}
    for c in range((2 * reach + 1) * rb):
        for g in range(rb):
            found = jnp.int32(zero_tile)
            for _, group, _, at, live, where in place:
                if group == g:
                    found = jnp.where(jnp.logical_and(live, where == c), at, found)
            inverse[c, g] = found
    tl_t[zero_tile] = jnp.zeros((fb, fb), BF16)

    loads[0].wait()
    loads[1].wait()
    total = dot(xall[f], w_ref[rows_of(f), :], ((1,), (0,)))
    for i, k in enumerate(steps):
        receive(0, i)
        total = total + dot(xall[k], w_ref[rows_of(k), :], ((1,), (0,)))
    yw[pl.ds(reach * rb, rb)] = total.astype(BF16).reshape(rb, fb, fw)
    y_in = [push(yw.at[pl.ds(reach * rb, rb)], yw.at[pl.ds((reach - o) * rb, rb)], "rows",
                 lax.rem(r + o + n, n)) for o in halo]
    for k in range(m):
        x_t[pl.ds(k * fw, fw), :] = xall[k].T
    for i in range(m - 2):
        for g in range(rb):
            receive(1 + g, i)
    for copy in y_in:
        copy.wait_recv()
    loads[2].wait()

    sums = [jnp.zeros((fb, fw), F32) for _ in range(rb)]
    def add(groups, first, last):
        for g in groups:
            mine = [p for p in place[first * per:last * per] if p[1] == g]
            tiles = [tl[at] for _, _, _, at, _, _ in mine]
            blocks = [jnp.where(live, yw[jnp.minimum(where, yw.shape[0] - 1)], jnp.zeros((), BF16))
                      for _, _, _, _, live, where in mine]
            sums[g] = sums[g] + dot(jnp.concatenate(tiles, axis=1), jnp.concatenate(blocks, axis=0), ((1,), (0,)))
            for tile, (_, _, _, at, _, _) in zip(tiles, mine):
                tl_t[at] = tile.T

    add(range(rb), 0, m - 1)
    for g in range(rb):
        receive(1 + g, m - 2)
        add([g], m - 1, m)
    w_in = [push(w_hbm.at[rows_of(lax.rem(f + d, m))], wrow.at[f], "feat", lax.rem(f + d, m)) for d in feat_d]
    pre = jnp.concatenate(sums, axis=0)
    hidden, slope = gelu_and_slope(pre)
    loads[3].wait()
    grad_pre = (ct_ref[...].astype(F32) * slope).astype(BF16)

    def spread(o, b):
        c = (reach + o) * rb + b
        tiles = jnp.concatenate([tl_t[inverse[c, g]] for g in range(rb)], axis=1)
        return dot(tiles, grad_pre, ((1,), (0,)))

    s_in = {}
    far_first = list(reversed(halo))
    for b in range(rb):
        for at, o in enumerate(far_first):
            sw[b, at] = spread(o, b).astype(BF16)
            s_in[b, at] = push(sw.at[b, at], sr.at[b, at], "rows", lax.rem(r + o + n, n))
    hid_ref[...] = hidden.astype(BF16)
    grads = [spread(0, b) for b in range(rb)]
    loads[4].wait()
    for copy in w_in:
        copy.wait_recv()
    for k in range(m):
        w_t[pl.ds(k * fw, fw), :] = wrow[k].T
    g_in = {}
    for b in range(rb):
        grad = grads[b]
        for at in range(len(far_first)):
            s_in[b, at].wait_recv()
            grad = grad + sr[b, at].astype(F32)
        grad = grad.astype(BF16)
        gall[b, f] = grad
        for d in feat_d:
            g_in[b, d] = push(gall.at[b, f], gall.at[b, f], "feat", lax.rem(f + d, m))
        grads[b] = grad
    terms = dot(x_t[...], jnp.concatenate(grads, axis=0), ((1,), (0,)))
    gwp[...] = terms.astype(BF16)
    gpart[...] = terms
    scale = float(rows * n) ** -0.5
    if in_sum:
        def chunk_of(d):
            return pl.ds(pl.multiple_of(lax.rem(r + n + d, n) * chunk, chunk), chunk)

        gw_in = {d: push(gwp.at[chunk_of(d)], gwr.at[d], "rows", lax.rem(r + d, n)) for d in row_d}
        part = gpart[chunk_of(0), :]
        for d in row_d:
            gw_in[d].wait_recv()
            part = part + gwr[d].astype(F32)
        own_sum = (part * scale).astype(BF16)
        gwa[0] = own_sum
        all_in = {d: push(gwa.at[0], gwa.at[d], "rows", lax.rem(r + d, n)) for d in row_d}
        gw_ref[chunk_of(0), :] = own_sum.astype(F32)
    else:
        gw_ref[...] = gpart[...] * scale

    for b in range(rb):
        for d in feat_d:
            g_in[b, d].wait_recv()
        out = dot(jnp.concatenate([gall[b, k] for k in range(m)], axis=1), w_t[...], ((1,), (0,)))
        gf_ref[pl.ds(b * fb, fb), :] = out.astype(BF16)
    if in_sum:
        for d in row_d:
            all_in[d].wait_recv()
            gw_ref[chunk_of(-d), :] = gwa[d].astype(F32)
    for copy in started:
        copy.wait_send()
    for sent, copy in forwards:
        pl.when(sent)(copy.wait_send)


def store_kernel(a, b, c, a_out, b_out, c_out, sem):
    copies = [pltpu.make_async_copy(src, dst, sem.at[i])
              for i, (src, dst) in enumerate(((c, c_out), (a, a_out), (b, b_out)))]
    for copy in copies:
        copy.start()
    for copy in copies:
        copy.wait()


def on_device(features, weight, block_values, columns, counts, cotangent):
    n = lax.axis_size("rows")
    m = lax.axis_size("feat")
    reach = min(4, (n - 1) // 3)
    rb, sl, fb, _ = block_values.shape
    rows, fw = features.shape
    depth = weight.shape[0]
    in_sum = depth % (n * 16) == 0
    chunk = depth // n if in_sum else 16
    span = 2 * reach + 1
    copies = (1 + rb) * (m - 1) + (1 + rb) * 2 * reach + (2 * (n - 1) if in_sum else 0)
    vmem = pl.BlockSpec(memory_space=pltpu.VMEM)
    hbm = pl.BlockSpec(memory_space=pltpu.HBM)
    hidden, grad_features, grad_weight = pl.pallas_call(
        functools.partial(kernel, n, m, reach, rb, sl, in_sum),
        out_shape=(
            pltpu.VMEM((rows, fw), BF16),
            pltpu.VMEM((rows, fw), BF16),
            pltpu.VMEM((depth, fw), F32),
        ),
        in_specs=[hbm, hbm, hbm, hbm, hbm, hbm],
        out_specs=(vmem, vmem, vmem),
        scratch_shapes=[
            pltpu.VMEM((m, rows, fw), BF16),
            pltpu.VMEM((depth, fw), BF16),
            pltpu.VMEM((rows, fw), BF16),
            pltpu.VMEM((m, fw, fw), BF16),
            pltpu.VMEM((m * fw, fw), BF16),
            pltpu.VMEM((m * rb * sl, fb, fb), BF16),
            pltpu.VMEM((m * rb * sl + 1, fb, fb), BF16),
            pltpu.VMEM((m * fw, rows), BF16),
            pltpu.VMEM((span * rb, fb, fw), BF16),
            pltpu.VMEM((rb, 2 * reach, fb, fw), BF16),
            pltpu.VMEM((rb, 2 * reach, fb, fw), BF16),
            pltpu.VMEM((rb, m, fb, fw), BF16),
            pltpu.VMEM((depth, fw), F32),
            pltpu.VMEM((depth, fw), BF16),
            pltpu.VMEM((n if in_sum else 1, chunk, fw), BF16),
            pltpu.VMEM((n if in_sum else 1, chunk, fw), BF16),
            pltpu.SemaphoreType.DMA((copies,)),
            pltpu.SemaphoreType.DMA((copies,)),
            pltpu.SemaphoreType.DMA((1 + rb, 2 * m)),
            pltpu.SemaphoreType.DMA((1 + rb, m)),
            pltpu.SemaphoreType.DMA((7,)),
            pltpu.SMEM(columns.shape, jnp.int32),
            pltpu.SMEM(counts.shape, jnp.int32),
        ],
        compiler_params=pltpu.CompilerParams(
            collective_id=0, has_side_effects=True, vmem_limit_bytes=32 * 1024 * 1024),
    )(*(pltpu.with_memory_space_constraint(v, pltpu.HBM) for v in (
        columns, counts, features, weight, block_values.reshape(rb * sl, fb, fb), cotangent)))
    if not in_sum:
        grad_weight = lax.psum(grad_weight, "rows")
    results = (hidden, grad_features, grad_weight)
    return pl.pallas_call(
        store_kernel,
        out_shape=tuple(jax.ShapeDtypeStruct(v.shape, v.dtype) for v in results),
        in_specs=[vmem] * 3,
        out_specs=(hbm,) * 3,
        scratch_shapes=[pltpu.SemaphoreType.DMA((3,))],
        compiler_params=pltpu.CompilerParams(vmem_limit_bytes=32 * 1024 * 1024),
    )(*results)


def solution(mesh):
    in_specs = (
        P("rows", "feat"),
        P(None, "feat"),
        P("rows", "feat", None, None),
        P("rows", None),
        P("rows"),
        P("rows", "feat"),
    )
    out_specs = (P("rows", "feat"), P("rows", "feat"), P(None, "feat"))
    return jax.shard_map(
        on_device, mesh=mesh, in_specs=in_specs, out_specs=out_specs, check_vma=False
    )
```

```python
import functools

import jax
import jax.numpy as jnp
from jax import lax
from jax.experimental import pallas as pl
from jax.experimental.pallas import tpu as pltpu
from jax.sharding import PartitionSpec as P

MESH = pl.DeviceIdType.MESH
F32 = jnp.float32
BF16 = jnp.bfloat16
GELU_SCALE = 0.7978845608028654
GELU_CUBE = 0.044715


def gelu_and_slope(v):
    square = v * v
    t = jnp.tanh(GELU_SCALE * (v + GELU_CUBE * (square * v)))
    half = 0.5 * (1.0 + t)
    inner = GELU_SCALE * (1.0 + 3.0 * GELU_CUBE * square)
    return v * half, half + 0.5 * v * (1.0 - t * t) * inner


def dot(a, b, contract):
    return lax.dot_general(a, b, (contract, ((), ())), preferred_element_type=F32)


def nearest_first(f, m):
    tables = []
    for me in range(m):
        line = [p for e in range(1, m) for p in (me - e, me + e) if 0 <= p < m]
        tables.append(line)
    steps = []
    for i in range(m - 1):
        at = jnp.int32(tables[0][i])
        for me in range(1, m):
            at = jnp.where(f == me, tables[me][i], at)
        steps.append(at)
    return steps


def kernel(n, m, reach, rb, sl, in_sum, cols_hbm, cnt_hbm, x_hbm, w_hbm, t_hbm, ct_hbm,
           hid_ref, gf_ref, gw_ref, xall, w_ref, ct_ref, wrow, w_t, tl, tl_t, x_t, yw, sw, sr, gall, gpart, gwp, gwr, gwa,
           send_sem, recv_sem, hop_send, hop_recv, load_sem, cols, cnt):

    r = lax.axis_index("rows")
    f = lax.axis_index("feat")
    fb = t_hbm.shape[1]
    rows, fw = x_hbm.shape
    per = rb * sl
    chunk = gwr.shape[1]
    halo = [o for d in range(1, reach + 1) for o in (d, -d)]
    feat_d = list(range(1, m))
    row_d = list(range(1, n)) if in_sum else []
    row_peers = [d % n for d in (row_d if in_sum else halo)]

    def shard(s):
        return tl.at[pl.ds(s * per, per)]

    def rows_of(s):
        return pl.ds(pl.multiple_of(s * fw, fw), fw)

    loads = [
        pltpu.make_async_copy(x_hbm, xall.at[f], load_sem.at[0]),
        pltpu.make_async_copy(w_hbm, w_ref, load_sem.at[1]),
        pltpu.make_async_copy(t_hbm, shard(f), load_sem.at[2]),
        pltpu.make_async_copy(ct_hbm, ct_ref, load_sem.at[3]),
        pltpu.make_async_copy(w_hbm.at[rows_of(f)], wrow.at[f], load_sem.at[4]),
        pltpu.make_async_copy(cols_hbm, cols, load_sem.at[5]),
        pltpu.make_async_copy(cnt_hbm, cnt, load_sem.at[6]),
    ]
    for load in loads:
        load.start()

    barrier = pltpu.get_barrier_semaphore()
    for d in feat_d:
        pl.semaphore_signal(barrier, inc=1, device_id={"feat": lax.rem(f + d, m)}, device_id_type=MESH)
    for d in row_peers:
        pl.semaphore_signal(barrier, inc=1, device_id={"rows": lax.rem(r + d, n)}, device_id_type=MESH)
    pl.semaphore_wait(barrier, len(feat_d) + len(row_peers))

    started = []

    def push(src, dst, axis, peer):
        at = len(started)
        copy = pltpu.make_async_remote_copy(
            src_ref=src, dst_ref=dst, send_sem=send_sem.at[at], recv_sem=recv_sem.at[at],
            device_id={axis: peer}, device_id_type=MESH)
        copy.start()
        started.append(copy)
        return copy

    def slot_of(kind, s):
        return tl.at[pl.ds((s * rb + kind - 1) * sl, sl)] if kind else xall.at[s]

    def hop(kind, src, s, at, peer):
        return pltpu.make_async_remote_copy(
            src_ref=src, dst_ref=slot_of(kind, s), send_sem=hop_send.at[kind, at],
            recv_sem=hop_recv.at[kind, s], device_id={"feat": peer}, device_id_type=MESH)

    forwards = []

    def onward(kind, src, s, at, to_right, to_left):
        right = hop(kind, src, s, at, lax.rem(f + 1, m))
        left = hop(kind, src, s, at + 1, lax.rem(f + m - 1, m))
        pl.when(to_right)(right.start)
        pl.when(to_left)(left.start)
        forwards.append((to_right, right))
        forwards.append((to_left, left))

    for kind, src in enumerate([x_hbm] + [t_hbm.at[pl.ds(g * sl, sl)] for g in range(rb)]):
        onward(kind, src, f, 0, f < m - 1, f > 0)
    steps = nearest_first(f, m)

    def receive(kind, i):
        s = steps[i]
        hop(kind, slot_of(kind, s), s, 0, lax.rem(f + 1, m)).wait_recv()
        onward(kind, slot_of(kind, s), s, 2 + 2 * i, jnp.logical_and(s < f, f < m - 1),
               jnp.logical_and(s > f, f > 0))

    loads[0].wait()
    loads[1].wait()
    total = dot(xall[f], w_ref[rows_of(f), :], ((1,), (0,)))
    for i, k in enumerate(steps):
        receive(0, i)
        total = total + dot(xall[k], w_ref[rows_of(k), :], ((1,), (0,)))
    yw[pl.ds(reach * rb, rb)] = total.astype(BF16).reshape(rb, fb, fw)
    y_in = [push(yw.at[pl.ds(reach * rb, rb)], yw.at[pl.ds((reach - o) * rb, rb)], "rows",
                 lax.rem(r + o + n, n)) for o in halo]
    loads[5].wait()
    loads[6].wait()
    zero_tile = m * per
    order = [f] + steps
    place = []
    for s in order:
        for g in range(rb):
            for j in range(sl):
                slot = s * sl + j
                col = cols[g, slot]
                offset = lax.rem(lax.div(col, rb) - r + reach + n, n)
                live = cnt[g] > slot
                where = offset * rb + lax.rem(col, rb)
                place.append((s, g, j, (s * rb + g) * sl + j, live, where))
    inverse = {}
    for c in range((2 * reach + 1) * rb):
        for g in range(rb):
            found = jnp.int32(zero_tile)
            for _, group, _, at, live, where in place:
                if group == g:
                    found = jnp.where(jnp.logical_and(live, where == c), at, found)
            inverse[c, g] = found
    tl_t[zero_tile] = jnp.zeros((fb, fb), BF16)

    for i in range(m - 2):
        for g in range(rb):
            receive(1 + g, i)
    for copy in y_in:
        copy.wait_recv()
    loads[2].wait()

    sums = [jnp.zeros((fb, fw), F32) for _ in range(rb)]
    def add(groups, first, last):
        for g in groups:
            mine = [p for p in place[first * per:last * per] if p[1] == g]
            tiles = [tl[at] for _, _, _, at, _, _ in mine]
            blocks = [jnp.where(live, yw[jnp.minimum(where, yw.shape[0] - 1)], jnp.zeros((), BF16))
                      for _, _, _, _, live, where in mine]
            sums[g] = sums[g] + dot(jnp.concatenate(tiles, axis=1), jnp.concatenate(blocks, axis=0), ((1,), (0,)))
            for tile, (_, _, _, at, _, _) in zip(tiles, mine):
                tl_t[at] = tile.T

    add(range(rb), 0, m - 1)
    for g in range(rb):
        receive(1 + g, m - 2)
        add([g], m - 1, m)
    w_in = [push(w_hbm.at[rows_of(lax.rem(f + d, m))], wrow.at[f], "feat", lax.rem(f + d, m)) for d in feat_d]
    pre = jnp.concatenate(sums, axis=0)
    hidden, slope = gelu_and_slope(pre)
    loads[3].wait()
    grad_pre = (ct_ref[...].astype(F32) * slope).astype(BF16)

    def spread(o, b):
        c = (reach + o) * rb + b
        tiles = jnp.concatenate([tl_t[inverse[c, g]] for g in range(rb)], axis=1)
        return dot(tiles, grad_pre, ((1,), (0,)))

    s_in = []
    for at, o in enumerate(reversed(halo)):
        for b in range(rb):
            sw[at, pl.ds(b * fb, fb), :] = spread(o, b).astype(BF16)
        s_in.append(push(sw.at[at], sr.at[at], "rows", lax.rem(r + o + n, n)))
    grad = jnp.concatenate([spread(0, b) for b in range(rb)], axis=0)
    hid_ref[...] = hidden.astype(BF16)
    for k in range(m):
        x_t[pl.ds(k * fw, fw), :] = xall[k].T
    loads[4].wait()
    for copy in w_in:
        copy.wait_recv()
    for k in range(m):
        w_t[pl.ds(k * fw, fw), :] = wrow[k].T
    for at, copy in enumerate(s_in):
        copy.wait_recv()
        grad = grad + sr[at].astype(F32)
    grad = grad.astype(BF16)
    gall[f] = grad
    terms = dot(x_t[...], grad, ((1,), (0,)))
    gwp[...] = terms.astype(BF16)
    gpart[...] = terms

    def gather_grad():
        return [push(gall.at[f], gall.at[f], "feat", lax.rem(f + d, m)) for d in feat_d]

    scale = float(rows * n) ** -0.5
    if in_sum:
        def chunk_of(d):
            return pl.ds(pl.multiple_of(lax.rem(r + n + d, n) * chunk, chunk), chunk)

        gw_in = {d: push(gwp.at[chunk_of(d)], gwr.at[d], "rows", lax.rem(r + d, n)) for d in row_d}
        g_in = gather_grad()
        part = gpart[chunk_of(0), :]
        for d in row_d:
            gw_in[d].wait_recv()
            part = part + gwr[d].astype(F32)
        own_sum = (part * scale).astype(BF16)
        gwa[0] = own_sum
        all_in = {d: push(gwa.at[0], gwa.at[d], "rows", lax.rem(r + d, n)) for d in row_d}
        gw_ref[chunk_of(0), :] = own_sum.astype(F32)
    else:
        gw_ref[...] = gpart[...] * scale
        g_in = gather_grad()

    for copy in g_in:
        copy.wait_recv()
    out = dot(jnp.concatenate([gall[k] for k in range(m)], axis=1), w_t[...], ((1,), (0,)))
    gf_ref[...] = out.astype(BF16)
    if in_sum:
        for d in row_d:
            all_in[d].wait_recv()
            gw_ref[chunk_of(-d), :] = gwa[d].astype(F32)
    for copy in started:
        copy.wait_send()
    for sent, copy in forwards:
        pl.when(sent)(copy.wait_send)


def store_kernel(a, b, c, a_out, b_out, c_out, sem):
    copies = [pltpu.make_async_copy(src, dst, sem.at[i])
              for i, (src, dst) in enumerate(((c, c_out), (a, a_out), (b, b_out)))]
    for copy in copies:
        copy.start()
    for copy in copies:
        copy.wait()


def on_device(features, weight, block_values, columns, counts, cotangent):
    n = lax.axis_size("rows")
    m = lax.axis_size("feat")
    reach = min(4, (n - 1) // 3)
    rb, sl, fb, _ = block_values.shape
    rows, fw = features.shape
    depth = weight.shape[0]
    in_sum = depth % (n * 16) == 0
    chunk = depth // n if in_sum else 16
    span = 2 * reach + 1
    copies = 2 * (m - 1) + 4 * reach + (2 * (n - 1) if in_sum else 0)
    vmem = pl.BlockSpec(memory_space=pltpu.VMEM)
    hbm = pl.BlockSpec(memory_space=pltpu.HBM)
    hidden, grad_features, grad_weight = pl.pallas_call(
        functools.partial(kernel, n, m, reach, rb, sl, in_sum),
        out_shape=(
            pltpu.VMEM((rows, fw), BF16),
            pltpu.VMEM((rows, fw), BF16),
            pltpu.VMEM((depth, fw), F32),
        ),
        in_specs=[hbm, hbm, hbm, hbm, hbm, hbm],
        out_specs=(vmem, vmem, vmem),
        scratch_shapes=[
            pltpu.VMEM((m, rows, fw), BF16),
            pltpu.VMEM((depth, fw), BF16),
            pltpu.VMEM((rows, fw), BF16),
            pltpu.VMEM((m, fw, fw), BF16),
            pltpu.VMEM((m * fw, fw), BF16),
            pltpu.VMEM((m * rb * sl, fb, fb), BF16),
            pltpu.VMEM((m * rb * sl + 1, fb, fb), BF16),
            pltpu.VMEM((m * fw, rows), BF16),
            pltpu.VMEM((span * rb, fb, fw), BF16),
            pltpu.VMEM((2 * reach, rows, fw), BF16),
            pltpu.VMEM((2 * reach, rows, fw), BF16),
            pltpu.VMEM((m, rows, fw), BF16),
            pltpu.VMEM((depth, fw), F32),
            pltpu.VMEM((depth, fw), BF16),
            pltpu.VMEM((n if in_sum else 1, chunk, fw), BF16),
            pltpu.VMEM((n if in_sum else 1, chunk, fw), BF16),
            pltpu.SemaphoreType.DMA((copies,)),
            pltpu.SemaphoreType.DMA((copies,)),
            pltpu.SemaphoreType.DMA((1 + rb, 2 * m)),
            pltpu.SemaphoreType.DMA((1 + rb, m)),
            pltpu.SemaphoreType.DMA((7,)),
            pltpu.SMEM(columns.shape, jnp.int32),
            pltpu.SMEM(counts.shape, jnp.int32),
        ],
        compiler_params=pltpu.CompilerParams(
            collective_id=0, has_side_effects=True, vmem_limit_bytes=32 * 1024 * 1024),
    )(*(pltpu.with_memory_space_constraint(v, pltpu.HBM) for v in (
        columns, counts, features, weight, block_values.reshape(rb * sl, fb, fb), cotangent)))
    if not in_sum:
        grad_weight = lax.psum(grad_weight, "rows")
    results = (hidden, grad_features, grad_weight)
    return pl.pallas_call(
        store_kernel,
        out_shape=tuple(jax.ShapeDtypeStruct(v.shape, v.dtype) for v in results),
        in_specs=[vmem] * 3,
        out_specs=(hbm,) * 3,
        scratch_shapes=[pltpu.SemaphoreType.DMA((3,))],
        compiler_params=pltpu.CompilerParams(vmem_limit_bytes=32 * 1024 * 1024),
    )(*results)


def solution(mesh):
    in_specs = (
        P("rows", "feat"),
        P(None, "feat"),
        P("rows", "feat", None, None),
        P("rows", None),
        P("rows"),
        P("rows", "feat"),
    )
    out_specs = (P("rows", "feat"), P("rows", "feat"), P(None, "feat"))
    return jax.shard_map(
        on_device, mesh=mesh, in_specs=in_specs, out_specs=out_specs, check_vma=False
    )
```

```python
import functools

import jax
import jax.numpy as jnp
from jax import lax
from jax.experimental import pallas as pl
from jax.experimental.pallas import tpu as pltpu
from jax.sharding import PartitionSpec as P

MESH = pl.DeviceIdType.MESH
F32 = jnp.float32
BF16 = jnp.bfloat16
GELU_SCALE = 0.7978845608028654
GELU_CUBE = 0.044715


def gelu_and_slope(v):
    square = v * v
    t = jnp.tanh(GELU_SCALE * (v + GELU_CUBE * (square * v)))
    half = 0.5 * (1.0 + t)
    inner = GELU_SCALE * (1.0 + 3.0 * GELU_CUBE * square)
    return v * half, half + 0.5 * v * (1.0 - t * t) * inner


def dot(a, b, contract):
    return lax.dot_general(a, b, (contract, ((), ())), preferred_element_type=F32)


def nearest_first(f, m):
    tables = []
    for me in range(m):
        line = [p for e in range(1, m) for p in (me - e, me + e) if 0 <= p < m]
        tables.append(line)
    steps = []
    for i in range(m - 1):
        at = jnp.int32(tables[0][i])
        for me in range(1, m):
            at = jnp.where(f == me, tables[me][i], at)
        steps.append(at)
    return steps


def kernel(n, m, reach, rb, sl, in_sum, cols_hbm, cnt_hbm, x_hbm, w_hbm, t_hbm, ct_hbm,
           hid_ref, gf_ref, gw_ref, xall, w_ref, ct_ref, wrow, w_t, tl, tl_t, x_t, yw, sw, sr, gall, gpart, gwp, gwr, gwa,
           send_sem, recv_sem, hop_send, hop_recv, load_sem, cols, cnt):

    r = lax.axis_index("rows")
    f = lax.axis_index("feat")
    fb = t_hbm.shape[1]
    rows, fw = x_hbm.shape
    per = rb * sl
    chunk = gwr.shape[1]
    halo = [o for d in range(1, reach + 1) for o in (d, -d)]
    feat_d = list(range(1, m))
    row_d = list(range(1, n)) if in_sum else []
    row_peers = [d % n for d in (row_d if in_sum else halo)]

    def shard(s):
        return tl.at[pl.ds(s * per, per)]

    def rows_of(s):
        return pl.ds(pl.multiple_of(s * fw, fw), fw)

    loads = [
        pltpu.make_async_copy(x_hbm, xall.at[f], load_sem.at[0]),
        pltpu.make_async_copy(w_hbm, w_ref, load_sem.at[1]),
        pltpu.make_async_copy(t_hbm, shard(f), load_sem.at[2]),
        pltpu.make_async_copy(ct_hbm, ct_ref, load_sem.at[3]),
        pltpu.make_async_copy(w_hbm.at[rows_of(f)], wrow.at[f], load_sem.at[4]),
        pltpu.make_async_copy(cols_hbm, cols, load_sem.at[5]),
        pltpu.make_async_copy(cnt_hbm, cnt, load_sem.at[6]),
    ]
    for load in loads:
        load.start()

    barrier = pltpu.get_barrier_semaphore()
    for d in feat_d:
        pl.semaphore_signal(barrier, inc=1, device_id={"feat": lax.rem(f + d, m)}, device_id_type=MESH)
    for d in row_peers:
        pl.semaphore_signal(barrier, inc=1, device_id={"rows": lax.rem(r + d, n)}, device_id_type=MESH)
    pl.semaphore_wait(barrier, len(feat_d) + len(row_peers))

    started = []

    def push(src, dst, axis, peer):
        at = len(started)
        copy = pltpu.make_async_remote_copy(
            src_ref=src, dst_ref=dst, send_sem=send_sem.at[at], recv_sem=recv_sem.at[at],
            device_id={axis: peer}, device_id_type=MESH)
        copy.start()
        started.append(copy)
        return copy

    def slot_of(kind, s):
        return tl.at[pl.ds((s * rb + kind - 1) * sl, sl)] if kind else xall.at[s]

    def hop(kind, src, s, at, peer):
        return pltpu.make_async_remote_copy(
            src_ref=src, dst_ref=slot_of(kind, s), send_sem=hop_send.at[kind, at],
            recv_sem=hop_recv.at[kind, s], device_id={"feat": peer}, device_id_type=MESH)

    forwards = []

    def onward(kind, src, s, at, to_right, to_left):
        right = hop(kind, src, s, at, lax.rem(f + 1, m))
        left = hop(kind, src, s, at + 1, lax.rem(f + m - 1, m))
        pl.when(to_right)(right.start)
        pl.when(to_left)(left.start)
        forwards.append((to_right, right))
        forwards.append((to_left, left))

    for kind, src in enumerate([x_hbm] + [t_hbm.at[pl.ds(g * sl, sl)] for g in range(rb)]):
        onward(kind, src, f, 0, f < m - 1, f > 0)
    steps = nearest_first(f, m)

    def receive(kind, i):
        s = steps[i]
        hop(kind, slot_of(kind, s), s, 0, lax.rem(f + 1, m)).wait_recv()
        onward(kind, slot_of(kind, s), s, 2 + 2 * i, jnp.logical_and(s < f, f < m - 1),
               jnp.logical_and(s > f, f > 0))

    loads[0].wait()
    loads[1].wait()
    total = dot(xall[f], w_ref[rows_of(f), :], ((1,), (0,)))
    for i, k in enumerate(steps):
        receive(0, i)
        total = total + dot(xall[k], w_ref[rows_of(k), :], ((1,), (0,)))
    yw[pl.ds(reach * rb, rb)] = total.astype(BF16).reshape(rb, fb, fw)
    y_in = [push(yw.at[pl.ds(reach * rb, rb)], yw.at[pl.ds((reach - o) * rb, rb)], "rows",
                 lax.rem(r + o + n, n)) for o in halo]
    loads[5].wait()
    loads[6].wait()
    zero_tile = m * per
    order = [f] + steps
    place = []
    for s in order:
        for g in range(rb):
            for j in range(sl):
                slot = s * sl + j
                col = cols[g, slot]
                offset = lax.rem(lax.div(col, rb) - r + reach + n, n)
                live = cnt[g] > slot
                where = offset * rb + lax.rem(col, rb)
                place.append((s, g, j, (s * rb + g) * sl + j, live, where))
    inverse = {}
    for c in range((2 * reach + 1) * rb):
        for g in range(rb):
            found = jnp.int32(zero_tile)
            for _, group, _, at, live, where in place:
                if group == g:
                    found = jnp.where(jnp.logical_and(live, where == c), at, found)
            inverse[c, g] = found
    tl_t[zero_tile] = jnp.zeros((fb, fb), BF16)

    for i in range(m - 2):
        for g in range(rb):
            receive(1 + g, i)
    loads[2].wait()

    def transpose(first, last):
        for _, _, _, at, _, _ in place[first * per:last * per]:
            tl_t[at] = tl[at].T

    transpose(0, m - 1)
    for copy in y_in:
        copy.wait_recv()

    sums = [jnp.zeros((fb, fw), F32) for _ in range(rb)]
    def add(groups, first, last):
        for g in groups:
            mine = [p for p in place[first * per:last * per] if p[1] == g]
            tiles = [tl[at] for _, _, _, at, _, _ in mine]
            blocks = [jnp.where(live, yw[jnp.minimum(where, yw.shape[0] - 1)], jnp.zeros((), BF16))
                      for _, _, _, _, live, where in mine]
            sums[g] = sums[g] + dot(jnp.concatenate(tiles, axis=1), jnp.concatenate(blocks, axis=0), ((1,), (0,)))

    add(range(rb), 0, m - 1)
    for g in range(rb):
        receive(1 + g, m - 2)
        add([g], m - 1, m)
    transpose(m - 1, m)
    w_in = [push(w_hbm.at[rows_of(lax.rem(f + d, m))], wrow.at[f], "feat", lax.rem(f + d, m)) for d in feat_d]
    pre = jnp.concatenate(sums, axis=0)
    hidden, slope = gelu_and_slope(pre)
    loads[3].wait()
    grad_pre = (ct_ref[...].astype(F32) * slope).astype(BF16)

    def spread(o, b):
        c = (reach + o) * rb + b
        tiles = jnp.concatenate([tl_t[inverse[c, g]] for g in range(rb)], axis=1)
        return dot(tiles, grad_pre, ((1,), (0,)))

    s_in = []
    for at, o in enumerate(reversed(halo)):
        for b in range(rb):
            sw[at, pl.ds(b * fb, fb), :] = spread(o, b).astype(BF16)
        s_in.append(push(sw.at[at], sr.at[at], "rows", lax.rem(r + o + n, n)))
    grad = jnp.concatenate([spread(0, b) for b in range(rb)], axis=0)
    hid_ref[...] = hidden.astype(BF16)
    for k in range(m):
        x_t[pl.ds(k * fw, fw), :] = xall[k].T
    loads[4].wait()
    for copy in w_in:
        copy.wait_recv()
    for k in range(m):
        w_t[pl.ds(k * fw, fw), :] = wrow[k].T
    for at, copy in enumerate(s_in):
        copy.wait_recv()
        grad = grad + sr[at].astype(F32)
    grad = grad.astype(BF16)
    gall[f] = grad
    terms = dot(x_t[...], grad, ((1,), (0,)))
    gwp[...] = terms.astype(BF16)
    gpart[...] = terms

    def gather_grad():
        return [push(gall.at[f], gall.at[f], "feat", lax.rem(f + d, m)) for d in feat_d]

    scale = float(rows * n) ** -0.5
    if in_sum:
        def chunk_of(d):
            return pl.ds(pl.multiple_of(lax.rem(r + n + d, n) * chunk, chunk), chunk)

        gw_in = {d: push(gwp.at[chunk_of(d)], gwr.at[d], "rows", lax.rem(r + d, n)) for d in row_d}
        g_in = gather_grad()
        part = gpart[chunk_of(0), :]
        for d in row_d:
            gw_in[d].wait_recv()
            part = part + gwr[d].astype(F32)
        own_sum = (part * scale).astype(BF16)
        gwa[0] = own_sum
        all_in = {d: push(gwa.at[0], gwa.at[d], "rows", lax.rem(r + d, n)) for d in row_d}
        gw_ref[chunk_of(0), :] = own_sum.astype(F32)
    else:
        gw_ref[...] = gpart[...] * scale
        g_in = gather_grad()

    for copy in g_in:
        copy.wait_recv()
    out = dot(jnp.concatenate([gall[k] for k in range(m)], axis=1), w_t[...], ((1,), (0,)))
    gf_ref[...] = out.astype(BF16)
    if in_sum:
        for d in row_d:
            all_in[d].wait_recv()
            gw_ref[chunk_of(-d), :] = gwa[d].astype(F32)
    for copy in started:
        copy.wait_send()
    for sent, copy in forwards:
        pl.when(sent)(copy.wait_send)


def store_kernel(a, b, c, a_out, b_out, c_out, sem):
    copies = [pltpu.make_async_copy(src, dst, sem.at[i])
              for i, (src, dst) in enumerate(((c, c_out), (a, a_out), (b, b_out)))]
    for copy in copies:
        copy.start()
    for copy in copies:
        copy.wait()


def on_device(features, weight, block_values, columns, counts, cotangent):
    n = lax.axis_size("rows")
    m = lax.axis_size("feat")
    reach = min(4, (n - 1) // 3)
    rb, sl, fb, _ = block_values.shape
    rows, fw = features.shape
    depth = weight.shape[0]
    in_sum = depth % (n * 16) == 0
    chunk = depth // n if in_sum else 16
    span = 2 * reach + 1
    copies = 2 * (m - 1) + 4 * reach + (2 * (n - 1) if in_sum else 0)
    vmem = pl.BlockSpec(memory_space=pltpu.VMEM)
    hbm = pl.BlockSpec(memory_space=pltpu.HBM)
    hidden, grad_features, grad_weight = pl.pallas_call(
        functools.partial(kernel, n, m, reach, rb, sl, in_sum),
        out_shape=(
            pltpu.VMEM((rows, fw), BF16),
            pltpu.VMEM((rows, fw), BF16),
            pltpu.VMEM((depth, fw), F32),
        ),
        in_specs=[hbm, hbm, hbm, hbm, hbm, hbm],
        out_specs=(vmem, vmem, vmem),
        scratch_shapes=[
            pltpu.VMEM((m, rows, fw), BF16),
            pltpu.VMEM((depth, fw), BF16),
            pltpu.VMEM((rows, fw), BF16),
            pltpu.VMEM((m, fw, fw), BF16),
            pltpu.VMEM((m * fw, fw), BF16),
            pltpu.VMEM((m * rb * sl, fb, fb), BF16),
            pltpu.VMEM((m * rb * sl + 1, fb, fb), BF16),
            pltpu.VMEM((m * fw, rows), BF16),
            pltpu.VMEM((span * rb, fb, fw), BF16),
            pltpu.VMEM((2 * reach, rows, fw), BF16),
            pltpu.VMEM((2 * reach, rows, fw), BF16),
            pltpu.VMEM((m, rows, fw), BF16),
            pltpu.VMEM((depth, fw), F32),
            pltpu.VMEM((depth, fw), BF16),
            pltpu.VMEM((n if in_sum else 1, chunk, fw), BF16),
            pltpu.VMEM((n if in_sum else 1, chunk, fw), BF16),
            pltpu.SemaphoreType.DMA((copies,)),
            pltpu.SemaphoreType.DMA((copies,)),
            pltpu.SemaphoreType.DMA((1 + rb, 2 * m)),
            pltpu.SemaphoreType.DMA((1 + rb, m)),
            pltpu.SemaphoreType.DMA((7,)),
            pltpu.SMEM(columns.shape, jnp.int32),
            pltpu.SMEM(counts.shape, jnp.int32),
        ],
        compiler_params=pltpu.CompilerParams(
            collective_id=0, has_side_effects=True, vmem_limit_bytes=32 * 1024 * 1024),
    )(*(pltpu.with_memory_space_constraint(v, pltpu.HBM) for v in (
        columns, counts, features, weight, block_values.reshape(rb * sl, fb, fb), cotangent)))
    if not in_sum:
        grad_weight = lax.psum(grad_weight, "rows")
    results = (hidden, grad_features, grad_weight)
    return pl.pallas_call(
        store_kernel,
        out_shape=tuple(jax.ShapeDtypeStruct(v.shape, v.dtype) for v in results),
        in_specs=[vmem] * 3,
        out_specs=(hbm,) * 3,
        scratch_shapes=[pltpu.SemaphoreType.DMA((3,))],
        compiler_params=pltpu.CompilerParams(vmem_limit_bytes=32 * 1024 * 1024),
    )(*results)


def solution(mesh):
    in_specs = (
        P("rows", "feat"),
        P(None, "feat"),
        P("rows", "feat", None, None),
        P("rows", None),
        P("rows"),
        P("rows", "feat"),
    )
    out_specs = (P("rows", "feat"), P("rows", "feat"), P(None, "feat"))
    return jax.shard_map(
        on_device, mesh=mesh, in_specs=in_specs, out_specs=out_specs, check_vma=False
    )
```

```python
import functools

import jax
import jax.numpy as jnp
from jax import lax
from jax.experimental import pallas as pl
from jax.experimental.pallas import tpu as pltpu
from jax.sharding import PartitionSpec as P

MESH = pl.DeviceIdType.MESH
F32 = jnp.float32
BF16 = jnp.bfloat16
GELU_SCALE = 0.7978845608028654
GELU_CUBE = 0.044715


def gelu_and_slope(v):
    square = v * v
    t = jnp.tanh(GELU_SCALE * (v + GELU_CUBE * (square * v)))
    half = 0.5 * (1.0 + t)
    inner = GELU_SCALE * (1.0 + 3.0 * GELU_CUBE * square)
    return v * half, half + 0.5 * v * (1.0 - t * t) * inner


def dot(a, b, contract):
    return lax.dot_general(a, b, (contract, ((), ())), preferred_element_type=F32)


def nearest_first(f, m):
    tables = []
    for me in range(m):
        line = [p for e in range(1, m) for p in (me - e, me + e) if 0 <= p < m]
        tables.append(line)
    steps = []
    for i in range(m - 1):
        at = jnp.int32(tables[0][i])
        for me in range(1, m):
            at = jnp.where(f == me, tables[me][i], at)
        steps.append(at)
    return steps


def kernel(n, m, reach, rb, sl, in_sum, cols_hbm, cnt_hbm, x_hbm, w_hbm, t_hbm, ct_hbm,
           hid_ref, gf_ref, gw_ref, xall, w_ref, ct_ref, wrow, w_t, tl, tl_t, x_t, yw, sw, sr, gall, gpart, gwp, gwr, gwa,
           send_sem, recv_sem, hop_send, hop_recv, load_sem, cols, cnt):

    r = lax.axis_index("rows")
    f = lax.axis_index("feat")
    fb = t_hbm.shape[1]
    rows, fw = x_hbm.shape
    per = rb * sl
    chunk = gwr.shape[1]
    halo = [o for d in range(1, reach + 1) for o in (d, -d)]
    feat_d = list(range(1, m))
    row_d = list(range(1, n)) if in_sum else []
    row_peers = [d % n for d in (row_d if in_sum else halo)]

    def shard(s):
        return tl.at[pl.ds(s * per, per)]

    def rows_of(s):
        return pl.ds(pl.multiple_of(s * fw, fw), fw)

    loads = [
        pltpu.make_async_copy(x_hbm, xall.at[f], load_sem.at[0]),
        pltpu.make_async_copy(w_hbm, w_ref, load_sem.at[1]),
        pltpu.make_async_copy(t_hbm, shard(f), load_sem.at[2]),
        pltpu.make_async_copy(ct_hbm, ct_ref, load_sem.at[3]),
        pltpu.make_async_copy(w_hbm.at[rows_of(f)], wrow.at[f], load_sem.at[4]),
        pltpu.make_async_copy(cols_hbm, cols, load_sem.at[5]),
        pltpu.make_async_copy(cnt_hbm, cnt, load_sem.at[6]),
    ]
    for load in loads:
        load.start()

    barrier = pltpu.get_barrier_semaphore()
    for d in feat_d:
        pl.semaphore_signal(barrier, inc=1, device_id={"feat": lax.rem(f + d, m)}, device_id_type=MESH)
    for d in row_peers:
        pl.semaphore_signal(barrier, inc=1, device_id={"rows": lax.rem(r + d, n)}, device_id_type=MESH)
    pl.semaphore_wait(barrier, len(feat_d) + len(row_peers))

    started = []

    def push(src, dst, axis, peer):
        at = len(started)
        copy = pltpu.make_async_remote_copy(
            src_ref=src, dst_ref=dst, send_sem=send_sem.at[at], recv_sem=recv_sem.at[at],
            device_id={axis: peer}, device_id_type=MESH)
        copy.start()
        started.append(copy)
        return copy

    def slot_of(kind, s):
        return tl.at[pl.ds((s * rb + kind - 1) * sl, sl)] if kind else xall.at[s]

    def hop(kind, src, s, at, peer):
        return pltpu.make_async_remote_copy(
            src_ref=src, dst_ref=slot_of(kind, s), send_sem=hop_send.at[kind, at],
            recv_sem=hop_recv.at[kind, s], device_id={"feat": peer}, device_id_type=MESH)

    forwards = []

    def onward(kind, src, s, at, to_right, to_left):
        right = hop(kind, src, s, at, lax.rem(f + 1, m))
        left = hop(kind, src, s, at + 1, lax.rem(f + m - 1, m))
        pl.when(to_right)(right.start)
        pl.when(to_left)(left.start)
        forwards.append((to_right, right))
        forwards.append((to_left, left))

    own = list(enumerate([x_hbm] + [t_hbm.at[pl.ds(g * sl, sl)] for g in range(rb)]))
    for kind, src in own[1:2] + own[:1] + own[2:]:
        onward(kind, src, f, 0, f < m - 1, f > 0)
    steps = nearest_first(f, m)

    def receive(kind, i):
        s = steps[i]
        hop(kind, slot_of(kind, s), s, 0, lax.rem(f + 1, m)).wait_recv()
        onward(kind, slot_of(kind, s), s, 2 + 2 * i, jnp.logical_and(s < f, f < m - 1),
               jnp.logical_and(s > f, f > 0))

    loads[0].wait()
    loads[1].wait()
    total = dot(xall[f], w_ref[rows_of(f), :], ((1,), (0,)))
    for i, k in enumerate(steps):
        receive(0, i)
        total = total + dot(xall[k], w_ref[rows_of(k), :], ((1,), (0,)))
    yw[pl.ds(reach * rb, rb)] = total.astype(BF16).reshape(rb, fb, fw)
    y_in = [push(yw.at[pl.ds(reach * rb, rb)], yw.at[pl.ds((reach - o) * rb, rb)], "rows",
                 lax.rem(r + o + n, n)) for o in halo]
    loads[5].wait()
    loads[6].wait()
    zero_tile = m * per
    order = [f] + steps
    place = []
    for s in order:
        for g in range(rb):
            for j in range(sl):
                slot = s * sl + j
                col = cols[g, slot]
                offset = lax.rem(lax.div(col, rb) - r + reach + n, n)
                live = cnt[g] > slot
                where = offset * rb + lax.rem(col, rb)
                place.append((s, g, j, (s * rb + g) * sl + j, live, where))
    inverse = {}
    for c in range((2 * reach + 1) * rb):
        for g in range(rb):
            found = jnp.int32(zero_tile)
            for _, group, _, at, live, where in place:
                if group == g:
                    found = jnp.where(jnp.logical_and(live, where == c), at, found)
            inverse[c, g] = found
    tl_t[zero_tile] = jnp.zeros((fb, fb), BF16)

    for i in range(m - 2):
        for g in range(rb):
            receive(1 + g, i)
    loads[2].wait()

    def transpose(first, last):
        for _, _, _, at, _, _ in place[first * per:last * per]:
            tl_t[at] = tl[at].T

    transpose(0, m - 1)
    for copy in y_in:
        copy.wait_recv()

    sums = [jnp.zeros((fb, fw), F32) for _ in range(rb)]
    def add(groups, first, last):
        for g in groups:
            mine = [p for p in place[first * per:last * per] if p[1] == g]
            tiles = [tl[at] for _, _, _, at, _, _ in mine]
            blocks = [jnp.where(live, yw[jnp.minimum(where, yw.shape[0] - 1)], jnp.zeros((), BF16))
                      for _, _, _, _, live, where in mine]
            sums[g] = sums[g] + dot(jnp.concatenate(tiles, axis=1), jnp.concatenate(blocks, axis=0), ((1,), (0,)))

    add(range(rb), 0, m - 1)
    for g in range(rb):
        receive(1 + g, m - 2)
        add([g], m - 1, m)
    transpose(m - 1, m)
    w_in = [push(w_hbm.at[rows_of(lax.rem(f + d, m))], wrow.at[f], "feat", lax.rem(f + d, m)) for d in feat_d]
    pre = jnp.concatenate(sums, axis=0)
    hidden, slope = gelu_and_slope(pre)
    loads[3].wait()
    grad_pre = (ct_ref[...].astype(F32) * slope).astype(BF16)

    def spread(o, b):
        c = (reach + o) * rb + b
        tiles = jnp.concatenate([tl_t[inverse[c, g]] for g in range(rb)], axis=1)
        return dot(tiles, grad_pre, ((1,), (0,)))

    s_in = []
    for at, o in enumerate(reversed(halo)):
        for b in range(rb):
            sw[at, pl.ds(b * fb, fb), :] = spread(o, b).astype(BF16)
        s_in.append(push(sw.at[at], sr.at[at], "rows", lax.rem(r + o + n, n)))
    grad = jnp.concatenate([spread(0, b) for b in range(rb)], axis=0)
    hid_ref[...] = hidden.astype(BF16)
    for k in range(m):
        x_t[pl.ds(k * fw, fw), :] = xall[k].T
    loads[4].wait()
    for copy in w_in:
        copy.wait_recv()
    for k in range(m):
        w_t[pl.ds(k * fw, fw), :] = wrow[k].T
    for at, copy in enumerate(s_in):
        copy.wait_recv()
        grad = grad + sr[at].astype(F32)
    grad = grad.astype(BF16)
    gall[f] = grad
    terms = dot(x_t[...], grad, ((1,), (0,)))
    gwp[...] = terms.astype(BF16)
    gpart[...] = terms

    def gather_grad():
        return [push(gall.at[f], gall.at[f], "feat", lax.rem(f + d, m)) for d in feat_d]

    scale = float(rows * n) ** -0.5
    if in_sum:
        def chunk_of(d):
            return pl.ds(pl.multiple_of(lax.rem(r + n + d, n) * chunk, chunk), chunk)

        gw_in = {d: push(gwp.at[chunk_of(d)], gwr.at[d], "rows", lax.rem(r + d, n)) for d in row_d}
        g_in = gather_grad()
        part = gpart[chunk_of(0), :]
        for d in row_d:
            gw_in[d].wait_recv()
            part = part + gwr[d].astype(F32)
        own_sum = (part * scale).astype(BF16)
        gwa[0] = own_sum
        all_in = {d: push(gwa.at[0], gwa.at[d], "rows", lax.rem(r + d, n)) for d in row_d}
        gw_ref[chunk_of(0), :] = own_sum.astype(F32)
    else:
        gw_ref[...] = gpart[...] * scale
        g_in = gather_grad()

    for copy in g_in:
        copy.wait_recv()
    out = dot(jnp.concatenate([gall[k] for k in range(m)], axis=1), w_t[...], ((1,), (0,)))
    gf_ref[...] = out.astype(BF16)
    if in_sum:
        for d in row_d:
            all_in[d].wait_recv()
            gw_ref[chunk_of(-d), :] = gwa[d].astype(F32)
    for copy in started:
        copy.wait_send()
    for sent, copy in forwards:
        pl.when(sent)(copy.wait_send)


def store_kernel(a, b, c, a_out, b_out, c_out, sem):
    copies = [pltpu.make_async_copy(src, dst, sem.at[i])
              for i, (src, dst) in enumerate(((c, c_out), (a, a_out), (b, b_out)))]
    for copy in copies:
        copy.start()
    for copy in copies:
        copy.wait()


def on_device(features, weight, block_values, columns, counts, cotangent):
    n = lax.axis_size("rows")
    m = lax.axis_size("feat")
    reach = min(4, (n - 1) // 3)
    rb, sl, fb, _ = block_values.shape
    rows, fw = features.shape
    depth = weight.shape[0]
    in_sum = depth % (n * 16) == 0
    chunk = depth // n if in_sum else 16
    span = 2 * reach + 1
    copies = 2 * (m - 1) + 4 * reach + (2 * (n - 1) if in_sum else 0)
    vmem = pl.BlockSpec(memory_space=pltpu.VMEM)
    hbm = pl.BlockSpec(memory_space=pltpu.HBM)
    hidden, grad_features, grad_weight = pl.pallas_call(
        functools.partial(kernel, n, m, reach, rb, sl, in_sum),
        out_shape=(
            pltpu.VMEM((rows, fw), BF16),
            pltpu.VMEM((rows, fw), BF16),
            pltpu.VMEM((depth, fw), F32),
        ),
        in_specs=[hbm, hbm, hbm, hbm, hbm, hbm],
        out_specs=(vmem, vmem, vmem),
        scratch_shapes=[
            pltpu.VMEM((m, rows, fw), BF16),
            pltpu.VMEM((depth, fw), BF16),
            pltpu.VMEM((rows, fw), BF16),
            pltpu.VMEM((m, fw, fw), BF16),
            pltpu.VMEM((m * fw, fw), BF16),
            pltpu.VMEM((m * rb * sl, fb, fb), BF16),
            pltpu.VMEM((m * rb * sl + 1, fb, fb), BF16),
            pltpu.VMEM((m * fw, rows), BF16),
            pltpu.VMEM((span * rb, fb, fw), BF16),
            pltpu.VMEM((2 * reach, rows, fw), BF16),
            pltpu.VMEM((2 * reach, rows, fw), BF16),
            pltpu.VMEM((m, rows, fw), BF16),
            pltpu.VMEM((depth, fw), F32),
            pltpu.VMEM((depth, fw), BF16),
            pltpu.VMEM((n if in_sum else 1, chunk, fw), BF16),
            pltpu.VMEM((n if in_sum else 1, chunk, fw), BF16),
            pltpu.SemaphoreType.DMA((copies,)),
            pltpu.SemaphoreType.DMA((copies,)),
            pltpu.SemaphoreType.DMA((1 + rb, 2 * m)),
            pltpu.SemaphoreType.DMA((1 + rb, m)),
            pltpu.SemaphoreType.DMA((7,)),
            pltpu.SMEM(columns.shape, jnp.int32),
            pltpu.SMEM(counts.shape, jnp.int32),
        ],
        compiler_params=pltpu.CompilerParams(
            collective_id=0, has_side_effects=True, vmem_limit_bytes=32 * 1024 * 1024),
    )(*(pltpu.with_memory_space_constraint(v, pltpu.HBM) for v in (
        columns, counts, features, weight, block_values.reshape(rb * sl, fb, fb), cotangent)))
    if not in_sum:
        grad_weight = lax.psum(grad_weight, "rows")
    results = (hidden, grad_features, grad_weight)
    return pl.pallas_call(
        store_kernel,
        out_shape=tuple(jax.ShapeDtypeStruct(v.shape, v.dtype) for v in results),
        in_specs=[vmem] * 3,
        out_specs=(hbm,) * 3,
        scratch_shapes=[pltpu.SemaphoreType.DMA((3,))],
        compiler_params=pltpu.CompilerParams(vmem_limit_bytes=32 * 1024 * 1024),
    )(*results)


def solution(mesh):
    in_specs = (
        P("rows", "feat"),
        P(None, "feat"),
        P("rows", "feat", None, None),
        P("rows", None),
        P("rows"),
        P("rows", "feat"),
    )
    out_specs = (P("rows", "feat"), P("rows", "feat"), P(None, "feat"))
    return jax.shard_map(
        on_device, mesh=mesh, in_specs=in_specs, out_specs=out_specs, check_vma=False
    )
```
